256 devices in a mesh: inp: 4 (over z_hi), out: 8 (over y, core), dep: 8 (over z_lo, x).
Axes of the slice: x: 4, y: 4, z: 8 (z_hi: 4, z_lo: 2; z = z_hi * 2 + z_lo), core: 2. Of those that a mesh axis runs over, the one named last changes fastest.
Arguments:
- tokens: bfloat16 [3072, 6144], P(('dep', 'out'), 'inp'), may hold values from -6 to 6
- cotangent: bfloat16 [3072, 6144], P(('dep', 'out'), 'inp'), may hold values from -16 to 16
- weight_in: bfloat16 [6144, 12288], P(('inp', 'dep'), 'out'), may hold values from -0.078125 to 0.078125
- weight_out: bfloat16 [12288, 6144], P(('out', 'dep'), 'inp'), may hold values from -0.0546875 to 0.0546875
Outputs:
- tokens_grad: bfloat16 [3072, 6144], P(('dep', 'out'), 'inp')
- weight_in_grad: bfloat16 [6144, 12288], P(('inp', 'dep'), 'out')
- weight_out_grad: bfloat16 [12288, 6144], P(('out', 'dep'), 'inp')
The draws below stay inside these ranges and needn't reach their ends.
All inputs are finite; a program needn't handle non-finite values.
Results may differ from the reference program's by a relative error of at most 0.025.
Values may be sent and summed in bfloat16 or wider, within the bound.
A program may use at most 64 MiB of HBM per device.

```python
import jax
import jax.numpy as jnp
from jax import lax

D = 6144
FF = 12288
TOK_DEV = 384
TOKENS = 3072
N_DEP = 8


def with_spikes(entries, stream_key, source, target, blocks, factor):
    owner, partner = [(jnp.arange(entries.shape[position]) // (entries.shape[position] // blocks)).reshape([-1 if axis == position else 1 for axis in range(entries.ndim)]) for position in (source, target)]
    chosen = jax.random.permutation(stream_key, blocks)[partner]
    strong = (owner == chosen) | (owner == (partner + blocks // 2) % blocks)
    return jnp.where(strong, factor * entries, entries)


def block_levels(stream_key, shape, shards, least, top_value):
    factor_of, own = 1.0, jax.random.fold_in(stream_key, 6)
    for dim, blocks in shards:
        steps = jnp.exp(jax.random.uniform(jax.random.fold_in(own, dim), (blocks,), jnp.float32, least / len(shards), top_value / len(shards)))
        factor_of = factor_of * jnp.repeat(steps, shape[dim] // blocks).reshape([-1 if axis == dim else 1 for axis in range(len(shape))])
    return factor_of


def centred(own_key, extent, spread, bound, shards=(), held_as=jnp.bfloat16):
    values = jax.random.normal(own_key, extent, jnp.float32) * spread
    if len(shards) > 0:
        values = block_levels(own_key, extent, shards, -0.22, 0.18) * values
    return jnp.clip(values, min=-bound, max=bound).astype(held_as)


def gaussian_with(key, shape, deviation, reach, shards, heavy, held_as=jnp.bfloat16):
    array = deviation * jax.random.normal(key, shape, jnp.float32)
    if shards:
        array = array * block_levels(key, shape, shards, -0.22, 0.18)
    return jnp.clip(with_spikes(array, jax.random.fold_in(key, 3), *heavy), -reach, reach).astype(held_as)


def setup_inputs(seed: int = 0) -> dict:
    splits = jax.random.split(jax.random.key(seed), 5)
    return {
        "tokens": centred(splits[0], (TOKENS, D), 1.0, 6.0, ((0, 64), (1, 4))),
        "cotangent": gaussian_with(splits[1], (TOKENS, D), 1.0, 16.0, ((0, 64), (1, 4)), (0, 1, 64, 4.0)),
        "weight_in": centred(splits[2], (D, FF), D ** -0.5, 0.078125, ((0, 32), (1, 8))),
        "weight_out": centred(splits[3], (FF, D), FF ** -0.5, 0.0546875, ((0, 64), (1, 4))),
    }


def gelu_parts(preact):
    normal_cdf = 0.5 * (1.0 + lax.erf(preact * 0.7071067811865476))
    density = jnp.exp(-0.5 * preact * preact) * 0.3989422804014327
    return preact * normal_cdf, normal_cdf + preact * density


def reference(tokens, cotangent, weight_in, weight_out):
    preact = jnp.dot(tokens, weight_in, preferred_element_type=jnp.float32)
    act_grad = jnp.dot(cotangent, weight_out.T, preferred_element_type=jnp.float32)
    values, slopes = gelu_parts(preact)
    hidden_act = values.astype(jnp.bfloat16)
    pre_grad = (act_grad * slopes).astype(jnp.bfloat16)
    tokens_grad = jnp.dot(pre_grad, weight_in.T, preferred_element_type=jnp.float32).astype(jnp.bfloat16)
    grad_scale = float(TOKENS) ** -0.5
    token_blocks = tokens.reshape(N_DEP, TOK_DEV, D)
    cotan_blocks = cotangent.reshape(N_DEP, TOK_DEV, D)
    pregrad_blocks = pre_grad.reshape(N_DEP, TOK_DEV, FF)
    hidden_blocks = hidden_act.reshape(N_DEP, TOK_DEV, FF)

    def accumulate(totals, block):
        token_rows, cotan_rows, pregrad_rows, hidden_rows = block
        in_term = (grad_scale * jnp.dot(token_rows.T, pregrad_rows, preferred_element_type=jnp.float32)).astype(jnp.bfloat16)
        out_term = (grad_scale * jnp.dot(hidden_rows.T, cotan_rows, preferred_element_type=jnp.float32)).astype(jnp.bfloat16)
        in_term, out_term = lax.optimization_barrier((in_term, out_term))
        return (totals[0] + in_term.astype(jnp.float32), totals[1] + out_term.astype(jnp.float32)), None

    start = (jnp.zeros((D, FF), jnp.float32), jnp.zeros((FF, D), jnp.float32))
    totals, unused = lax.scan(accumulate, start, (token_blocks, cotan_blocks, pregrad_blocks, hidden_blocks))
    return tokens_grad, totals[0].astype(jnp.bfloat16), totals[1].astype(jnp.bfloat16)
```

```python
import functools

import jax
import jax.numpy as jnp
from jax import lax
from jax.experimental import pallas as pl
from jax.experimental.pallas import tpu as pltpu
from jax.sharding import PartitionSpec as P

MESH = pl.DeviceIdType.MESH
BF16, F32 = jnp.bfloat16, jnp.float32
NJ, CH = 3, 256
ND, DC = 3, 512
TB, WB = 48, 192
TOK, WID, HID = 768, 1536, 768
OWN = 192


def dot(a, b, ca, cb):
    return lax.dot_general(a, b, (((ca,), (cb,)), ((), ())), preferred_element_type=F32)


def gelu_parts(preact):
    normal_cdf = 0.5 * (1.0 + lax.erf(preact * 0.7071067811865476))
    density = jnp.exp(-0.5 * preact * preact) * 0.3989422804014327
    return preact * normal_cdf, normal_cdf + preact * density


def kernel(
    scale, tok, cot, win, wout, o_tok, o_win, o_wout,
    tg, wi, wo, pf, ps, pr, hg, slope, dwof, dwos, dwor, dwif, dwis, dwir, dwcs, dwcr,
    dxf, dxss, dxsr, dxyf, dxys, dxyr, dxcs, dxcr,
    m_loc, m_agc, m_agy, m_ags, m_wic, m_wix, m_wox, m_rs, m_hg, m_dwo, m_dwi, m_dwc, m_dxs, m_dxy, m_dxc,
):
    k, out, dep = lax.axis_index("inp"), lax.axis_index("out"), lax.axis_index("dep")
    y, co, c, x = out // 2, out % 2, dep // 4, dep % 4
    oc, oco = 1 - c, 1 - co

    def dev(dk=0, dy=0, dx=0, fc=0, fs=0):
        o = (y + dy) % 4 * 2 + (oco if fs else co)
        d = (oc if fc else c) * 4 + (x + dx) % 4
        return {"inp": (k + dk) % 4, "out": o, "dep": d}

    def cp(src, dst, sem, idx, to):
        return pltpu.make_async_remote_copy(
            src_ref=src, dst_ref=dst, send_sem=sem.at[(0,) + idx], recv_sem=sem.at[(1,) + idx],
            device_id=to, device_id_type=MESH,
        )

    def rows(start, n):
        return pl.ds(pl.multiple_of(start, 16), n)

    def tslot(a, cc, yy, oo):
        return tg.at[a, rows(((cc * 4 + yy) * 2 + oo) * TB, TB)]

    def ag_c(a):
        return cp((tok, cot)[a], tslot(a, c, y, co), m_agc, (a,), dev(fc=1))

    def ag_y(a, p, dy):
        slot = tslot(a, oc if p else c, y, co)
        return cp(slot if p else (tok, cot)[a], slot, m_agy, (a, p, dy - 1), dev(dy=dy))

    def ag_s(a, p, dy):
        slot = tslot(a, oc if p else c, (y + 4 - dy) % 4, co)
        src = (tok, cot)[a] if (p == 0 and dy == 0) else slot
        return cp(src, slot, m_ags, (a, p, dy), dev(fs=1))

    def wslot(j, cc, xx):
        return wi.at[j, rows((cc * 4 + xx) * WB, WB)]

    def wcols(cc, j):
        return win.at[:, pl.ds(pl.multiple_of(cc * HID + j * CH, CH), CH)]

    def wi_c(j):
        return cp(wcols(oc, j), wslot(j, c, x), m_wic, (j,), dev(fc=1))

    def wi_x(j, p, dx):
        slot = wslot(j, oc if p else c, x)
        return cp(slot if p else wcols(c, j), slot, m_wix, (j, p, dx - 1), dev(dx=dx))

    def wo_x(dx):
        return cp(wout, wo.at[rows(x * WB, WB)], m_wox, (dx - 1,), dev(dx=dx))

    def rs(a, j, dz):
        return cp(ps.at[a, j, rows((k + dz) % 4 * OWN, OWN)], pr.at[a, j, dz - 1], m_rs, (a, j, dz - 1), dev(dk=dz))

    def ag_h(a, j, dz):
        slot = hg.at[a, j, rows(k * OWN, OWN)]
        return cp(slot, slot, m_hg, (a, j, dz - 1), dev(dk=dz))

    def dwo_x(dx):
        return cp(dwos.at[rows((x + dx) % 4 * WB, WB)], dwor.at[dx - 1], m_dwo, (dx - 1,), dev(dx=dx))

    def dwi_x(j, cc, dx):
        src = dwis.at[j, rows((cc * 4 + (x + dx) % 4) * WB, WB)]
        return cp(src, dwir.at[j, dx - 1, cc], m_dwi, (j, dx - 1, cc), dev(dx=dx))

    def dw_c(j):
        return cp(dwcs.at[j], dwcr.at[j], m_dwc, (j,), dev(fc=1))

    def dx_s(d):
        return cp(dxss.at[d], dxsr.at[d], m_dxs, (d,), dev(fs=1))

    def dx_y(d, dy):
        return cp(dxys.at[d, (y + dy) % 4], dxyr.at[d, dy - 1], m_dxy, (d, dy - 1), dev(dy=dy))

    def dx_c(d):
        return cp(dxcs.at[d], dxcr.at[d], m_dxc, (d,), dev(fc=1))

    local = [pltpu.make_async_copy((tok, cot)[a], tslot(a, c, y, co), m_loc.at[a]) for a in range(2)]
    local += [pltpu.make_async_copy(wcols(c, j), wslot(j, c, x), m_loc.at[2 + j]) for j in range(NJ)]
    local += [pltpu.make_async_copy(wout, wo.at[rows(x * WB, WB)], m_loc.at[5])]
    for copy in local:
        copy.start()
    barrier = pltpu.get_barrier_semaphore()
    partners = [dev(fs=1), dev(fc=1)]
    for d in (1, 2, 3):
        partners += [dev(dk=d), dev(dy=d), dev(dx=d)]
    for to in partners:
        pl.semaphore_signal(barrier, inc=1, device_id=to, device_id_type=MESH)
    pl.semaphore_wait(barrier, len(partners))

    wi_c(0).start()
    for d in (2, 1, 3):
        wi_x(0, 0, d).start()
        ag_y(0, 0, d).start()
    ag_c(0).start()
    ag_s(0, 0, 0).start()
    wi_c(1).start()
    wi_c(2).start()
    ag_c(1).start()
    wi_c(0).wait_recv()
    for d in (2, 1, 3):
        wi_x(0, 1, d).start()
    ag_c(0).wait_recv()
    for d in (2, 1, 3):
        ag_y(0, 1, d).start()
    ag_s(0, 1, 0).start()
    for j in (1, 2):
        for d in (2, 1, 3):
            wi_x(j, 0, d).start()
        wi_c(j).wait_recv()
        for d in (2, 1, 3):
            wi_x(j, 1, d).start()
    for d in (2, 1, 3):
        wo_x(d).start()
    for p in (0, 1):
        for d in (1, 3, 2):
            ag_y(0, p, d).wait_recv()
            ag_s(0, p, d).start()
    for d in (2, 1, 3):
        ag_y(1, 0, d).start()
    ag_s(1, 0, 0).start()
    ag_c(1).wait_recv()
    for d in (2, 1, 3):
        ag_y(1, 1, d).start()
    ag_s(1, 1, 0).start()
    for copy in local:
        copy.wait()
    for p in (0, 1):
        for d in range(4):
            ag_s(0, p, d).wait_recv()

    def product(a, j, value):
        pf[a, j] = value
        ps[a, j] = value.astype(BF16)
        for d in (2, 1, 3):
            rs(a, j, d).start()

    def total(a, j):
        for d in (1, 2, 3):
            rs(a, j, d).wait_recv()
        value = pf[a, j, rows(k * OWN, OWN)]
        for d in range(3):
            value = value + pr[a, j, d].astype(F32)
        return value

    def share(a, j, value):
        hg[a, j, rows(k * OWN, OWN)] = value.astype(BF16)
        for d in (2, 1, 3):
            ag_h(a, j, d).start()

    @pl.loop(0, NJ)
    def _(j):
        for p in (0, 1):
            for d in (1, 2, 3):
                wi_x(j, p, d).wait_recv()
        product(0, j, dot(tg[0], wi[j], 1, 0))

    for p in (0, 1):
        for d in (1, 3, 2):
            ag_y(1, p, d).wait_recv()
            ag_s(1, p, d).start()

    @pl.loop(0, NJ)
    def _(j):
        value, slope_j = gelu_parts(total(0, j))
        slope[j] = slope_j
        share(0, j, value)

    for p in (0, 1):
        for d in range(4):
            ag_s(1, p, d).wait_recv()
    for d in (1, 2, 3):
        wo_x(d).wait_recv()

    @pl.loop(0, NJ)
    def _(j):
        product(1, j, dot(tg[1], wo[rows(j * CH, CH)], 1, 1))

    @pl.loop(0, NJ)
    def _(j):
        for d in (1, 2, 3):
            ag_h(0, j, d).wait_recv()
        value = scale * dot(hg[0, j], tg[1], 0, 0)
        dwof[rows(j * CH, CH)] = value
        dwos[rows(j * CH, CH)] = value.astype(BF16)

    for d in (2, 1, 3):
        dwo_x(d).start()

    @pl.loop(0, NJ)
    def _(j):
        share(1, j, total(1, j) * slope[j])

    def weight_in_part(j):
        value = scale * dot(tg[0], hg[1, j], 0, 0)
        dwif[j] = value
        dwis[j] = value.astype(BF16)
        for d in (2, 1, 3):
            for cc in range(2):
                dwi_x(j, cc, d).start()

    def cols(d):
        return pl.ds(pl.multiple_of(d * DC, DC), DC)

    @pl.loop(0, NJ - 1)
    def _(j):
        for d in (1, 2, 3):
            ag_h(1, j, d).wait_recv()
        weight_in_part(j)

        @pl.loop(0, ND)
        def _(d):
            part = dot(hg[1, j], wi[j, cols(d)], 1, 1)

            @pl.when(j == 0)
            def _():
                dxf[d] = part

            @pl.when(j > 0)
            def _():
                dxf[d] += part

    for d in (1, 2, 3):
        dwo_x(d).wait_recv()
    value = dwof[rows(x * WB, WB)]
    for d in range(3):
        value = value + dwor[d].astype(F32)
    o_wout[...] = value.astype(BF16)

    for d in (1, 2, 3):
        ag_h(1, NJ - 1, d).wait_recv()

    @pl.loop(0, ND)
    def _(d):
        dxf[d] += dot(hg[1, NJ - 1], wi[NJ - 1, cols(d)], 1, 1)
        for b in range(8):
            dxss[d, b] = dxf[d, rows((b * 2 + oco) * TB, TB)].astype(BF16)
        dx_s(d).start()

    weight_in_part(NJ - 1)

    @pl.loop(0, ND)
    def _(d):
        dx_s(d).wait_recv()
        for cc in range(2):
            for yy in range(4):
                b = cc * 4 + yy
                part = dxf[d, rows((b * 2 + co) * TB, TB)] + dxsr[d, b].astype(F32)
                dxyf[d, yy, cc] = part
                dxys[d, yy, cc] = part.astype(BF16)
        for dy in (2, 1, 3):
            dx_y(d, dy).start()

    def weight_in_send(j):
        for d in (1, 2, 3):
            for cc in range(2):
                dwi_x(j, cc, d).wait_recv()
        value = dwif[j, rows((oc * 4 + x) * WB, WB)]
        for d in range(3):
            value = value + dwir[j, d, oc].astype(F32)
        dwcs[j] = value.astype(BF16)
        dw_c(j).start()
        value = dwif[j, rows((c * 4 + x) * WB, WB)]
        for d in range(3):
            value = value + dwir[j, d, c].astype(F32)
        o_win[:, pl.ds(pl.multiple_of(c * HID + j * CH, CH), CH)] = value.astype(BF16)

    @pl.loop(0, NJ - 1)
    def _(j):
        weight_in_send(j)

    @pl.loop(0, ND)
    def _(d):
        for dy in (1, 2, 3):
            dx_y(d, dy).wait_recv()
        value = dxyf[d, y, oc]
        for i in range(3):
            value = value + dxyr[d, i, oc].astype(F32)
        dxcs[d] = value.astype(BF16)
        dx_c(d).start()
        value = dxyf[d, y, c]
        for i in range(3):
            value = value + dxyr[d, i, c].astype(F32)
        dxyf[d, y, c] = value

    weight_in_send(NJ - 1)

    @pl.loop(0, ND)
    def _(d):
        dx_c(d).wait_recv()
        o_tok[:, cols(d)] = (dxyf[d, y, c] + dxcr[d].astype(F32)).astype(BF16)

    @pl.loop(0, NJ)
    def _(j):
        dw_c(j).wait_recv()
        o_win[:, pl.ds(pl.multiple_of(oc * HID + j * CH, CH), CH)] = dwcr[j]

    for a in range(2):
        ag_c(a).wait_send()
        for p in range(2):
            for d in (1, 2, 3):
                ag_y(a, p, d).wait_send()
            for d in range(4):
                ag_s(a, p, d).wait_send()
    for d in (1, 2, 3):
        wo_x(d).wait_send()
        dwo_x(d).wait_send()

    @pl.loop(0, NJ)
    def _(j):
        wi_c(j).wait_send()
        dw_c(j).wait_send()
        for d in (1, 2, 3):
            for p in range(2):
                wi_x(j, p, d).wait_send()
                dwi_x(j, p, d).wait_send()
                rs(p, j, d).wait_send()
                ag_h(p, j, d).wait_send()

    @pl.loop(0, ND)
    def _(d):
        dx_s(d).wait_send()
        dx_c(d).wait_send()
        for dy in (1, 2, 3):
            dx_y(d, dy).wait_send()


def shards(tokens, cotangent, weight_in, weight_out):
    scale = float(tokens.shape[0] * lax.axis_size("out") * lax.axis_size("dep")) ** (-0.5)
    vmem, dma = pltpu.VMEM, pltpu.SemaphoreType.DMA
    hbm = pl.BlockSpec(memory_space=pl.ANY)
    own = pl.BlockSpec(memory_space=pltpu.VMEM)
    return pl.pallas_call(
        functools.partial(kernel, scale),
        out_shape=tuple(jax.ShapeDtypeStruct(a.shape, BF16) for a in (tokens, weight_in, weight_out)),
        in_specs=[hbm] * 4,
        out_specs=(own,) * 3,
        scratch_shapes=[
            vmem((2, TOK, WID), BF16),
            vmem((NJ, WID, CH), BF16),
            vmem((HID, WID), BF16),
            vmem((2, NJ, TOK, CH), F32),
            vmem((2, NJ, TOK, CH), BF16),
            vmem((2, NJ, 3, OWN, CH), BF16),
            vmem((2, NJ, TOK, CH), BF16),
            vmem((NJ, OWN, CH), F32),
            vmem((HID, WID), F32),
            vmem((HID, WID), BF16),
            vmem((3, WB, WID), BF16),
            vmem((NJ, WID, CH), F32),
            vmem((NJ, WID, CH), BF16),
            vmem((NJ, 3, 2, WB, CH), BF16),
            vmem((NJ, WB, CH), BF16),
            vmem((NJ, WB, CH), BF16),
            vmem((ND, TOK, DC), F32),
            vmem((ND, 8, TB, DC), BF16),
            vmem((ND, 8, TB, DC), BF16),
            vmem((ND, 4, 2, TB, DC), F32),
            vmem((ND, 4, 2, TB, DC), BF16),
            vmem((ND, 3, 2, TB, DC), BF16),
            vmem((ND, TB, DC), BF16),
            vmem((ND, TB, DC), BF16),
            dma((6,)),
            dma((2, 2)),
            dma((2, 2, 2, 3)),
            dma((2, 2, 2, 4)),
            dma((2, NJ)),
            dma((2, NJ, 2, 3)),
            dma((2, 3)),
            dma((2, 2, NJ, 3)),
            dma((2, 2, NJ, 3)),
            dma((2, 3)),
            dma((2, NJ, 3, 2)),
            dma((2, NJ)),
            dma((2, ND)),
            dma((2, ND, 3)),
            dma((2, ND)),
        ],
        compiler_params=pltpu.CompilerParams(
            collective_id=0, has_side_effects=True, vmem_limit_bytes=61 * 2**20
        ),
        cost_estimate=pl.CostEstimate(flops=11 * 10**9, bytes_accessed=3 * 10**6, transcendentals=0),
    )(tokens, cotangent, weight_in, weight_out)


def solution(mesh):
    in_specs = (
        P(("dep", "out"), "inp"),
        P(("dep", "out"), "inp"),
        P(("inp", "dep"), "out"),
        P(("out", "dep"), "inp"),
    )
    out_specs = (P(("dep", "out"), "inp"), P(("inp", "dep"), "out"), P(("out", "dep"), "inp"))
    return jax.shard_map(shards, mesh=mesh, in_specs=in_specs, out_specs=out_specs, check_vma=False)
```

```python
import functools

import jax
import jax.numpy as jnp
from jax import lax
from jax.experimental import pallas as pl
from jax.experimental.pallas import tpu as pltpu
from jax.sharding import PartitionSpec as P

MESH = pl.DeviceIdType.MESH
BF16, F32 = jnp.bfloat16, jnp.float32
NJ, CH = 3, 256
NU = 2 * NJ
ND, DC = 2, 768
TB, WB = 48, 192
TOK, WID, HID = 768, 1536, 768
HALF, OWN = 384, 96


def dot(a, b, ca, cb):
    return lax.dot_general(a, b, (((ca,), (cb,)), ((), ())), preferred_element_type=F32)


def gelu_parts(preact):
    normal_cdf = 0.5 * (1.0 + lax.erf(preact * 0.7071067811865476))
    density = jnp.exp(-0.5 * preact * preact) * 0.3989422804014327
    return preact * normal_cdf, normal_cdf + preact * density


def kernel(
    scale, tok, cot, win, wout, o_tok, o_win, o_wout,
    tg, wi, wo, pf, s1s, s1r, s2s, s2r, hg, slope, dwof, dwos, dwor, dwif, dwis, dwir, dwcs, dwcr,
    dxf, dxss, dxsr, dxyf, dxys, dxyr, dxcs, dxcr,
    m_loc, sent, m_agc, m_agy, m_ags, m_wic, m_wix, m_wox, m_s1, m_s2, m_h1, m_h2, m_dwo, m_dwi, m_dwc, m_dxs, m_dxy, m_dxc,
):
    k, out, dep = lax.axis_index("inp"), lax.axis_index("out"), lax.axis_index("dep")
    y, co, c, x = out // 2, out % 2, dep // 4, dep % 4
    oc, oco = 1 - c, 1 - co
    half = (c, oc)

    def dev(dk=0, dy=0, dx=0, fc=0, fs=0):
        o = (y + dy) % 4 * 2 + (oco if fs else co)
        d = (oc if fc else c) * 4 + (x + dx) % 4
        return {"inp": (k + dk) % 4, "out": o, "dep": d}

    def cp(src, dst, family, recv, to):
        return pltpu.make_async_remote_copy(
            src_ref=src, dst_ref=dst, send_sem=sent.at[family], recv_sem=recv, device_id=to, device_id_type=MESH
        )

    def rows(start, n):
        return pl.ds(pl.multiple_of(start, 16), n)

    def tslot(a, cc, yy, oo):
        return tg.at[a, rows(((cc * 4 + yy) * 2 + oo) * TB, TB)]

    def ag_c(a):
        return cp((tok, cot)[a], tslot(a, c, y, co), 0, m_agc.at[a], dev(fc=1))

    def ag_y(a, p, dy):
        slot = tslot(a, half[p], y, co)
        return cp(slot if p else (tok, cot)[a], slot, 0, m_agy.at[a, p, dy - 1], dev(dy=dy))

    def ag_s(a, p, dy):
        slot = tslot(a, half[p], (y + 4 - dy) % 4, co)
        src = (tok, cot)[a] if (p == 0 and dy == 0) else slot
        return cp(src, slot, 0, m_ags.at[a, p], dev(fs=1))

    def ag_s_all(a, p):
        ref = tg.at[a, pl.ds(0, 4 * TB)]
        return cp(ref, ref, 0, m_ags.at[a, p], dev(fs=1))

    def wslot(j, cc, xx):
        return wi.at[j, rows((cc * 4 + xx) * WB, WB)]

    def wcols(cc, j):
        return win.at[:, pl.ds(pl.multiple_of(cc * HID + j * CH, CH), CH)]

    def wi_c(j):
        return cp(wcols(oc, j), wslot(j, c, x), 1, m_wic.at[j], dev(fc=1))

    def wi_x(j, p, dx):
        slot = wslot(j, half[p], x)
        return cp(slot if p else wcols(c, j), slot, 1, m_wix.at[j], dev(dx=dx))

    def wi_x_all(j):
        ref = wi.at[j, pl.ds(0, 6 * WB)]
        return cp(ref, ref, 1, m_wix.at[j], dev(dx=1))

    def wo_x(dx):
        return cp(wout, wo.at[rows(x * WB, WB)], 2, m_wox, dev(dx=dx))

    def wo_x_all():
        ref = wo.at[pl.ds(0, 3 * WB)]
        return cp(ref, ref, 2, m_wox, dev(dx=1))

    def unit(u):
        i = u % 6
        return (0, i // 2, i % 2) if u < 6 else (1, i % 3, 1 - i // 3)

    def s1(u, r):
        return cp(s1s.at[u, r], s1r.at[u, r], 3, m_s1.at[u, r], dev(dk=(1, 3)[r]))

    def s2(u, r):
        return cp(s2s.at[u, r], s2r.at[u, r], 4, m_s2.at[u, r], dev(dk=(1, 3)[r]))

    def hrows(u, owner, part, n):
        a, j, p = unit(u)
        return hg.at[a, j, rows(half[p] * HALF + owner % 4 * OWN + part * TB, n)]

    def h1(u, r):
        slot = hrows(u, k, 0, OWN)
        return cp(slot, slot, 5, m_h1.at[u, r], dev(dk=(1, 3)[r]))

    def h2(u, r):
        slot = hrows(u, k + (3, 1)[r], r, TB)
        return cp(slot, slot, 5, m_h2.at[u, r], dev(dk=(1, 3)[r]))

    def dwo_x(dx):
        return cp(dwos.at[rows((x + dx) % 4 * WB, WB)], dwor.at[dx - 1], 6, m_dwo, dev(dx=dx))

    def dwo_x_all():
        return cp(dwor, dwor, 6, m_dwo, dev(dx=1))

    def dwi_x(j, p, dx):
        src = dwis.at[j, rows((half[p] * 4 + (x + dx) % 4) * WB, WB)]
        return cp(src, dwir.at[j, p, dx - 1], 7, m_dwi.at[j, p], dev(dx=dx))

    def dwi_x_all(j, p):
        return cp(dwir.at[j, p], dwir.at[j, p], 7, m_dwi.at[j, p], dev(dx=1))

    def dw_c(j):
        return cp(dwcs.at[j], dwcr.at[j], 8, m_dwc.at[j], dev(fc=1))

    def dx_s(p, d):
        return cp(dxss.at[p, d], dxsr.at[p, d], 9, m_dxs.at[p, d], dev(fs=1))

    def dx_y(p, d, dy):
        return cp(dxys.at[p, d, (y + dy) % 4], dxyr.at[p, d, dy - 1], 10, m_dxy.at[p, d], dev(dy=dy))

    def dx_y_all(p, d):
        return cp(dxyr.at[p, d], dxyr.at[p, d], 10, m_dxy.at[p, d], dev(dy=1))

    def dx_c(d):
        return cp(dxcs.at[d], dxcr.at[d], 11, m_dxc.at[d], dev(fc=1))

    def product(u):
        a, j, p = unit(u)
        lhs = tg[a, rows(half[p] * HALF, HALF)]
        pf[u % 4] = dot(lhs, wo[rows(j * CH, CH)], 1, 1) if a else dot(lhs, wi[j], 1, 0)

        def piece(owner, part):
            return pf[u % 4, rows(owner % 4 * OWN + part * TB, TB)].astype(BF16)

        s1s[u, 0, 0] = piece(k + 2, 0)
        s1s[u, 0, 1] = piece(k + 1, 1)
        s1(u, 0).start()
        s1s[u, 1, 0] = piece(k + 2, 1)
        s1s[u, 1, 1] = piece(k + 3, 0)
        s1(u, 1).start()

    def middle(u):
        for r in range(2):
            s1(u, r).wait_recv()
            own = pf[u % 4, rows((k + (1, 3)[r]) % 4 * OWN + r * TB, TB)]
            s2s[u, r] = (own + s1r[u, r, 0].astype(F32)).astype(BF16)
            s2(u, r).start()

    def finish(u):
        a, j, p = unit(u)
        for r in range(2):
            s2(u, r).wait_recv()
            value = pf[u % 4, rows(k * OWN + r * TB, TB)] + s2r[u, r].astype(F32) + s1r[u, 1 - r, 1].astype(F32)
            if a:
                value = value * slope[j, p, r]
            else:
                value, slope[j, p, r] = gelu_parts(value)
            hg[a, j, rows(half[p] * HALF + k * OWN + r * TB, TB)] = value.astype(BF16)
        for r in range(2):
            h1(u, r).start()

    def forward(u):
        for r in range(2):
            h1(u, r).wait_recv()
            h2(u, r).start()

    def arrived(u):
        for r in range(2):
            h2(u, r).wait_recv()

    def weight_out_part():
        for j in range(NJ):
            value = scale * dot(hg[0, j], tg[1], 0, 0)
            dwof[rows(j * CH, CH)] = value
            dwos[rows(j * CH, CH)] = value.astype(BF16)
        for d in (2, 1, 3):
            dwo_x(d).start()

    def weight_out_finish():
        dwo_x_all().wait_recv()
        value = dwof[rows(x * WB, WB)]
        for d in range(3):
            value = value + dwor[d].astype(F32)
        o_wout[...] = value.astype(BF16)

    def weight_in_part(j):
        value = scale * dot(tg[0], hg[1, j], 0, 0)
        dwif[j] = value
        dwis[j] = value.astype(BF16)
        for p in (1, 0):
            for d in (2, 1, 3):
                dwi_x(j, p, d).start()

    def weight_in_sum(j, p):
        dwi_x_all(j, p).wait_recv()
        value = dwif[j, rows((half[p] * 4 + x) * WB, WB)]
        for d in range(3):
            value = value + dwir[j, p, d].astype(F32)
        if p:
            dwcs[j] = value.astype(BF16)
            dw_c(j).start()
        else:
            o_win[:, pl.ds(pl.multiple_of(c * HID + j * CH, CH), CH)] = value.astype(BF16)

    def weight_in_finish(j):
        dw_c(j).wait_recv()
        o_win[:, pl.ds(pl.multiple_of(oc * HID + j * CH, CH), CH)] = dwcr[j]

    def cols(d):
        return pl.ds(d * DC, DC)

    def tokens_part(p, j, d):
        part = dot(hg[1, j, rows(half[p] * HALF, HALF)], wi[j, cols(d)], 1, 1)
        if j == 0:
            dxf[p, d] = part
        else:
            dxf[p, d] += part
        if j == NJ - 1:
            for yy in range(4):
                dxss[p, d, yy] = dxf[p, d, rows((yy * 2 + oco) * TB, TB)].astype(BF16)
            dx_s(p, d).start()

    def tokens_middle(p, d):
        dx_s(p, d).wait_recv()
        for yy in range(4):
            part = dxf[p, d, rows((yy * 2 + co) * TB, TB)] + dxsr[p, d, yy].astype(F32)
            dxyf[p, d, yy] = part
            dxys[p, d, yy] = part.astype(BF16)
        for dy in (2, 1, 3):
            dx_y(p, d, dy).start()

    def tokens_sum(p, d):
        dx_y_all(p, d).wait_recv()
        value = dxyf[p, d, y]
        for i in range(3):
            value = value + dxyr[p, d, i].astype(F32)
        if p:
            dxcs[d] = value.astype(BF16)
            dx_c(d).start()
        else:
            dx_c(d).wait_recv()
            o_tok[:, cols(d)] = (value + dxcr[d].astype(F32)).astype(BF16)

    local = [pltpu.make_async_copy((tok, cot)[a], tslot(a, c, y, co), m_loc.at[a]) for a in range(2)]
    local += [pltpu.make_async_copy(wcols(c, j), wslot(j, c, x), m_loc.at[2 + j]) for j in range(NJ)]
    local += [pltpu.make_async_copy(wout, wo.at[rows(x * WB, WB)], m_loc.at[5])]
    for copy in local:
        copy.start()
    barrier = pltpu.get_barrier_semaphore()
    partners = [dev(fs=1), dev(fc=1), dev(dk=1), dev(dk=3)]
    for d in (1, 2, 3):
        partners += [dev(dy=d), dev(dx=d)]
    for to in partners:
        pl.semaphore_signal(barrier, inc=1, device_id=to, device_id_type=MESH)
    pl.semaphore_wait(barrier, len(partners))

    ag_c(0).start()
    for d in (2, 1, 3):
        ag_y(0, 0, d).start()
        wi_x(0, 0, d).start()
    wi_c(0).start()
    ag_s(0, 0, 0).start()
    wi_c(1).start()
    wi_c(2).start()
    ag_c(1).start()
    ag_c(0).wait_recv()
    for d in (2, 1, 3):
        ag_y(0, 1, d).start()
    ag_s(0, 1, 0).start()
    wi_c(0).wait_recv()
    for d in (2, 1, 3):
        wi_x(0, 1, d).start()
    for d in (2, 1, 3):
        wi_x(1, 0, d).start()
    for d in (1, 3, 2):
        ag_y(0, 0, d).wait_recv()
        ag_s(0, 0, d).start()
    wi_c(1).wait_recv()
    for d in (2, 1, 3):
        wi_x(1, 1, d).start()
    for copy in local:
        copy.wait()
    ag_s_all(0, 0).wait_recv()
    wi_x_all(0).wait_recv()
    product(0)
    for d in (1, 3, 2):
        ag_y(0, 1, d).wait_recv()
        ag_s(0, 1, d).start()
    for d in (2, 1, 3):
        ag_y(1, 0, d).start()
    ag_s(1, 0, 0).start()
    wi_c(2).wait_recv()
    for p in (0, 1):
        for d in (2, 1, 3):
            wi_x(2, p, d).start()
    ag_c(1).wait_recv()
    for d in (2, 1, 3):
        ag_y(1, 1, d).start()
    ag_s(1, 1, 0).start()
    ag_s_all(0, 1).wait_recv()

    for t in range(1, 2 * NU + 4):
        if t == 2:
            wi_x_all(1).wait_recv()
            for d in (2, 1, 3):
                wo_x(d).start()
        if t == 4:
            wi_x_all(2).wait_recv()
        if t == NU:
            wo_x_all().wait_recv()
            for p in (0, 1):
                ag_s_all(1, p).wait_recv()
        if t < 2 * NU:
            product(t)
        if 0 <= t - 1 < 2 * NU:
            middle(t - 1)
        if 0 <= t - 2 < 2 * NU:
            finish(t - 2)
        if 0 <= t - 3 < 2 * NU:
            forward(t - 3)
        if t == 4:
            for p in (0, 1):
                for d in (1, 3, 2):
                    ag_y(1, p, d).wait_recv()
                    ag_s(1, p, d).start()
        if t == NU + 3:
            for u in range(NU):
                arrived(u)
            weight_out_part()
        u = t - 4
        if u >= NU:
            a, j, p = unit(u)
            arrived(u)
            if p:
                for d in range(ND):
                    tokens_part(1, j, d)
            elif j < NJ - 1:
                weight_in_part(j)
                for d in range(ND):
                    tokens_part(0, j, d)
                for d in range(ND):
                    (tokens_middle, tokens_sum)[j](1, d)
    for d in range(ND):
        tokens_part(0, NJ - 1, d)
    weight_in_part(NJ - 1)
    for d in range(ND):
        tokens_middle(0, d)
    weight_out_finish()
    for j in range(NJ):
        weight_in_sum(j, 1)
        if j < NJ - 1:
            weight_in_sum(j, 0)
    for d in range(ND):
        tokens_sum(0, d)
    weight_in_sum(NJ - 1, 0)
    for j in range(NJ):
        weight_in_finish(j)

    whole = (
        tg.at[:, pl.ds(0, 15 * TB)], wi.at[:, pl.ds(0, 7 * WB)], wo.at[pl.ds(0, 3 * WB)], s1s, s2s,
        hg.at[:, :, pl.ds(0, 6 * OWN)], dwor, dwir, dwcs, dxss, dxyr, dxcs,
    )
    for family, ref in enumerate(whole):
        cp(ref, ref, family, m_agc.at[0], dev(fs=1)).wait_send()


def shards(tokens, cotangent, weight_in, weight_out):
    scale = float(tokens.shape[0] * lax.axis_size("out") * lax.axis_size("dep")) ** (-0.5)
    vmem, dma = pltpu.VMEM, pltpu.SemaphoreType.DMA
    hbm = pl.BlockSpec(memory_space=pl.ANY)
    own = pl.BlockSpec(memory_space=pltpu.VMEM)
    return pl.pallas_call(
        functools.partial(kernel, scale),
        out_shape=tuple(jax.ShapeDtypeStruct(a.shape, BF16) for a in (tokens, weight_in, weight_out)),
        in_specs=[hbm] * 4,
        out_specs=(own,) * 3,
        scratch_shapes=[
            vmem((2, TOK, WID), BF16),
            vmem((NJ, WID, CH), BF16),
            vmem((HID, WID), BF16),
            vmem((4, HALF, CH), F32),
            vmem((2 * NU, 2, 2, TB, CH), BF16),
            vmem((2 * NU, 2, 2, TB, CH), BF16),
            vmem((2 * NU, 2, TB, CH), BF16),
            vmem((2 * NU, 2, TB, CH), BF16),
            vmem((2, NJ, TOK, CH), BF16),
            vmem((NJ, 2, 2, TB, CH), F32),
            vmem((HID, WID), F32),
            vmem((HID, WID), BF16),
            vmem((3, WB, WID), BF16),
            vmem((NJ, WID, CH), F32),
            vmem((NJ, WID, CH), BF16),
            vmem((NJ, 2, 3, WB, CH), BF16),
            vmem((NJ, WB, CH), BF16),
            vmem((NJ, WB, CH), BF16),
            vmem((2, ND, HALF, DC), F32),
            vmem((2, ND, 4, TB, DC), BF16),
            vmem((2, ND, 4, TB, DC), BF16),
            vmem((2, ND, 4, TB, DC), F32),
            vmem((2, ND, 4, TB, DC), BF16),
            vmem((2, ND, 3, TB, DC), BF16),
            vmem((ND, TB, DC), BF16),
            vmem((ND, TB, DC), BF16),
            dma((6,)),
            dma((12,)),
            dma((2,)),
            dma((2, 2, 3)),
            dma((2, 2)),
            dma((NJ,)),
            dma((NJ,)),
            dma,
            dma((2 * NU, 2)),
            dma((2 * NU, 2)),
            dma((2 * NU, 2)),
            dma((2 * NU, 2)),
            dma,
            dma((NJ, 2)),
            dma((NJ,)),
            dma((2, ND)),
            dma((2, ND)),
            dma((ND,)),
        ],
        compiler_params=pltpu.CompilerParams(
            collective_id=0, has_side_effects=True, vmem_limit_bytes=61 * 2**20
        ),
        cost_estimate=pl.CostEstimate(flops=11 * 10**9, bytes_accessed=3 * 10**6, transcendentals=0),
    )(tokens, cotangent, weight_in, weight_out)


def solution(mesh):
    in_specs = (
        P(("dep", "out"), "inp"),
        P(("dep", "out"), "inp"),
        P(("inp", "dep"), "out"),
        P(("out", "dep"), "inp"),
    )
    out_specs = (P(("dep", "out"), "inp"), P(("inp", "dep"), "out"), P(("out", "dep"), "inp"))
    return jax.shard_map(shards, mesh=mesh, in_specs=in_specs, out_specs=out_specs, check_vma=False)
```

```python
import functools

import jax
import jax.numpy as jnp
from jax import lax
from jax.experimental import pallas as pl
from jax.experimental.pallas import tpu as pltpu
from jax.sharding import PartitionSpec as P

MESH = pl.DeviceIdType.MESH
BF16, F32 = jnp.bfloat16, jnp.float32
NJ, CH = 3, 256
NU = 2 * NJ
ND, DC = 2, 768
STEP = (1, 3)
TB, WB = 48, 192
TOK, WID, HID = 768, 1536, 768
HALF, OWN = 384, 96


def dot(a, b, ca, cb):
    return lax.dot_general(a, b, (((ca,), (cb,)), ((), ())), preferred_element_type=F32)


def gelu_parts(preact):
    normal_cdf = 0.5 * (1.0 + lax.erf(preact * 0.7071067811865476))
    density = jnp.exp(-0.5 * preact * preact) * 0.3989422804014327
    return preact * normal_cdf, normal_cdf + preact * density


def kernel(
    scale, tok, cot, win, wout, o_tok, o_win, o_wout,
    tg, wi, wo, pf, s1s, s1r, s2s, s2r, hg, slope, dwof, o1s, o1r, o2s, o2r,
    dwif, i1s, i1r, i2s, i2r, dwis, dwir, dwcs, dwcr, dxf, dxss, dxsr, dxyf, dxys, dxyr, dxcs, dxcr,
    r_tok, r_win, r_wout, m_loc, m_res, sent, m_agc, m_agy, m_ags, m_wic, m_wix, m_wif, m_wox, m_wof, m_s1, m_s2, m_h1, m_h2,
    m_o1, m_o2, m_i1, m_i2, m_dwi, m_dwc, m_dxs, m_dxy, m_dxc,
):
    k, out, dep = lax.axis_index("inp"), lax.axis_index("out"), lax.axis_index("dep")
    y, co, c, x = out // 2, out % 2, dep // 4, dep % 4
    oc, oco = 1 - c, 1 - co
    half = (c, oc)

    def dev(dk=0, dy=0, dx=0, fc=0, fs=0):
        o = (y + dy) % 4 * 2 + (oco if fs else co)
        d = (oc if fc else c) * 4 + (x + dx) % 4
        return {"inp": (k + dk) % 4, "out": o, "dep": d}

    def cp(src, dst, family, recv, to):
        return pltpu.make_async_remote_copy(
            src_ref=src, dst_ref=dst, send_sem=sent.at[family], recv_sem=recv, device_id=to, device_id_type=MESH
        )

    def rows(start, n):
        return pl.ds(pl.multiple_of(start, 16), n)

    def tslot(a, cc, yy, oo):
        return tg.at[a, rows(((cc * 4 + yy) * 2 + oo) * TB, TB)]

    def ag_c(a):
        return cp((tok, cot)[a], tslot(a, c, y, co), 0, m_agc.at[a], dev(fc=1))

    def ag_y(a, p, dy):
        slot = tslot(a, half[p], y, co)
        return cp(slot if p else (tok, cot)[a], slot, 0, m_agy.at[a, p, dy - 1], dev(dy=dy))

    def ag_s(a, p, dy):
        slot = tslot(a, half[p], (y + 4 - dy) % 4, co)
        src = (tok, cot)[a] if (p == 0 and dy == 0) else slot
        return cp(src, slot, 0, m_ags.at[a, p], dev(fs=1))

    def ag_s_all(a, p):
        ref = tg.at[a, pl.ds(0, 4 * TB)]
        return cp(ref, ref, 0, m_ags.at[a, p], dev(fs=1))

    def wslot(j, cc, xx):
        return wi.at[j, rows((cc * 4 + xx) * WB, WB)]

    def wcols(cc, j):
        return win.at[:, pl.ds(pl.multiple_of(cc * HID + j * CH, CH), CH)]

    def wi_c(j):
        return cp(wcols(oc, j), wslot(j, c, x), 1, m_wic.at[j], dev(fc=1))

    def wi_x(j, p, dx):
        slot = wslot(j, half[p], x)
        return cp(slot if p else wcols(c, j), slot, 1, m_wix.at[j], dev(dx=dx))

    def wi_x_all(j):
        ref = wi.at[j, pl.ds(0, (4 if j else 6) * WB)]
        return cp(ref, ref, 1, m_wix.at[j], dev(dx=1))

    def wi_n(j, p, r):
        slot = wslot(j, half[p], x)
        sem = m_wif.at[j, p] if p == r else m_wix.at[j]
        return cp(slot if p else wcols(c, j), slot, 1, sem, dev(dx=STEP[r]))

    def wi_f(j, p):
        slot = wslot(j, half[p], (x + STEP[1 - p]) % 4)
        return cp(slot, slot, 1, m_wix.at[j], dev(dx=STEP[p]))

    def wo_n(r):
        return cp(wout, wo.at[rows(x * WB, WB)], 2, m_wof.at[r], dev(dx=STEP[r]))

    def wo_f(r):
        slot = wo.at[rows((x + STEP[1 - r]) % 4 * WB + r * OWN, OWN)]
        return cp(slot, slot, 2, m_wox, dev(dx=STEP[r]))

    def wo_f_all():
        ref = wo.at[pl.ds(0, WB)]
        return cp(ref, ref, 2, m_wox, dev(dx=1))

    def unit(u):
        i = u % 6
        return (0, i // 2, i % 2) if u < 6 else (1, i % 3, 1 - i // 3)

    def s1(u, r):
        return cp(s1s.at[u, r], s1r.at[u, r], 3, m_s1.at[u, r], dev(dk=STEP[r]))

    def s2(u, r):
        return cp(s2s.at[u, r], s2r.at[u, r], 4, m_s2.at[u, r], dev(dk=STEP[r]))

    def hrows(u, owner, part, n):
        a, j, p = unit(u)
        return hg.at[a, j, rows(half[p] * HALF + owner % 4 * OWN + part * TB, n)]

    def h1(u, r):
        slot = hrows(u, k, 0, OWN)
        return cp(slot, slot, 5, m_h1.at[u, r], dev(dk=STEP[r]))

    def h2(u, r):
        slot = hrows(u, k + STEP[1 - r], r, TB)
        return cp(slot, slot, 5, m_h2.at[u, r], dev(dk=STEP[r]))

    def o1(r):
        return cp(o1s.at[r], o1r.at[r], 6, m_o1.at[r], dev(dx=STEP[r]))

    def o2(r):
        return cp(o2s.at[r], o2r.at[r], 7, m_o2.at[r], dev(dx=STEP[r]))

    def i1(j, r):
        return cp(i1s.at[j, r], i1r.at[j, r], 12, m_i1.at[j, r], dev(dx=STEP[r]))

    def i2(j, r):
        return cp(i2s.at[j, r], i2r.at[j, r], 13, m_i2.at[j, r], dev(dx=STEP[r]))

    def dwi_x(p, dx):
        return cp(dwis.at[p, dx - 1], dwir.at[p, dx - 1], 14, m_dwi.at[p], dev(dx=dx))

    def dwi_x_all(p):
        return cp(dwir.at[p], dwir.at[p], 14, m_dwi.at[p], dev(dx=1))

    def dw_c(j):
        return cp(dwcs.at[j], dwcr.at[j], 8, m_dwc.at[j], dev(fc=1))

    def dx_s(p, d):
        return cp(dxss.at[p, d], dxsr.at[p, d], 9, m_dxs.at[p, d], dev(fs=1))

    def dx_y(p, d, dy):
        return cp(dxys.at[p, d, (y + dy) % 4], dxyr.at[p, d, dy - 1], 10, m_dxy.at[p, d], dev(dy=dy))

    def dx_y_all(p, d):
        return cp(dxyr.at[p, d], dxyr.at[p, d], 10, m_dxy.at[p, d], dev(dy=1))

    def dx_c(d):
        return cp(dxcs.at[d], dxcr.at[d], 11, m_dxc.at[d], dev(fc=1))

    def product(u):
        a, j, p = unit(u)
        lhs = tg[a, rows(half[p] * HALF, HALF)]
        pf[u % 4] = dot(lhs, wo[rows(j * CH, CH)], 1, 1) if a else dot(lhs, wi[j], 1, 0)

        def piece(owner, part):
            return pf[u % 4, rows(owner % 4 * OWN + part * TB, TB)].astype(BF16)

        s1s[u, 0, 0] = piece(k + 2, 0)
        s1s[u, 0, 1] = piece(k + 1, 1)
        s1(u, 0).start()
        s1s[u, 1, 0] = piece(k + 2, 1)
        s1s[u, 1, 1] = piece(k + 3, 0)
        s1(u, 1).start()

    def middle(u):
        for r in range(2):
            s1(u, r).wait_recv()
            own = pf[u % 4, rows((k + STEP[r]) % 4 * OWN + r * TB, TB)]
            s2s[u, r] = (own + s1r[u, r, 0].astype(F32)).astype(BF16)
            s2(u, r).start()

    def finish(u):
        a, j, p = unit(u)
        for r in range(2):
            s2(u, r).wait_recv()
            value = pf[u % 4, rows(k * OWN + r * TB, TB)] + s2r[u, r].astype(F32) + s1r[u, 1 - r, 1].astype(F32)
            if a:
                value = value * slope[j, p, r]
            else:
                value, slope[j, p, r] = gelu_parts(value)
            hg[a, j, rows(half[p] * HALF + k * OWN + r * TB, TB)] = value.astype(BF16)
        for r in range(2):
            h1(u, r).start()

    def forward(u):
        for r in range(2):
            h1(u, r).wait_recv()
            h2(u, r).start()

    def arrived(u):
        for r in range(2):
            h2(u, r).wait_recv()

    def weight_out_part():
        for j in range(NJ):
            dwof[rows(j * CH, CH)] = scale * dot(hg[0, j], tg[1], 0, 0)

        def piece(owner, part):
            return dwof[rows(owner % 4 * WB + part * OWN, OWN)].astype(BF16)

        for r in range(2):
            o1s[r, 0] = piece(x + 2, r)
            o1s[r, 1] = piece(x + STEP[r], 1 - r)
            o1(r).start()

    def weight_out_middle():
        for r in range(2):
            o1(r).wait_recv()
            own = dwof[rows((x + STEP[r]) % 4 * WB + r * OWN, OWN)]
            o2s[r] = (own + o1r[r, 0].astype(F32)).astype(BF16)
            o2(r).start()

    def weight_out_finish():
        for r in range(2):
            o2(r).wait_recv()
            value = dwof[rows(x * WB + r * OWN, OWN)] + o2r[r].astype(F32) + o1r[1 - r, 1].astype(F32)
            r_wout[pl.ds(r * OWN, OWN)] = value.astype(BF16)
        result_out.start()

    def weight_in_half(j, p):
        value = scale * dot(tg[0, rows(half[p] * HALF, HALF)], hg[1, j, rows(half[p] * HALF, HALF)], 0, 0)
        if p:
            dwif[j] = value
        else:
            dwif[j] += value

    def weight_in_piece(j, p, owner):
        return dwif[j, rows((half[p] * 4 + owner % 4) * WB, WB)]

    def weight_in_part(j):
        weight_in_half(j, 0)
        if j == NJ - 1:
            for p in (1, 0):
                for d in (2, 1, 3):
                    dwis[p, d - 1] = weight_in_piece(j, p, x + d).astype(BF16)
                    dwi_x(p, d).start()
        else:
            for r in range(2):
                i1s[j, r, 0] = weight_in_piece(j, 1 - r, x + 2).astype(BF16)
                i1s[j, r, 1] = weight_in_piece(j, r, x + STEP[r]).astype(BF16)
                i1(j, r).start()

    def weight_in_middle(j):
        for r in range(2):
            i1(j, r).wait_recv()
            i2s[j, r] = (weight_in_piece(j, 1 - r, x + STEP[r]) + i1r[j, r, 0].astype(F32)).astype(BF16)
            i2(j, r).start()

    def weight_in_sum(j, p):
        value = weight_in_piece(j, p, x)
        if j == NJ - 1:
            dwi_x_all(p).wait_recv()
            for d in range(3):
                value = value + dwir[p, d].astype(F32)
        else:
            i2(j, 1 - p).wait_recv()
            value = value + i2r[j, 1 - p].astype(F32) + i1r[j, p, 1].astype(F32)
        if p:
            dwcs[j] = value.astype(BF16)
            dw_c(j).start()
        else:
            r_win[:, pl.ds(pl.multiple_of(c * HID + j * CH, CH), CH)] = value.astype(BF16)

    def weight_in_finish(j):
        dw_c(j).wait_recv()
        r_win[:, pl.ds(pl.multiple_of(oc * HID + j * CH, CH), CH)] = dwcr[j]

    def cols(d):
        return pl.ds(d * DC, DC)

    def tokens_part(p, j, d):
        part = dot(hg[1, j, rows(half[p] * HALF, HALF)], wi[j, cols(d)], 1, 1)
        if j == 0:
            dxf[p, d] = part
        else:
            dxf[p, d] += part
        if j == NJ - 1:
            for yy in range(4):
                dxss[p, d, yy] = dxf[p, d, rows((yy * 2 + oco) * TB, TB)].astype(BF16)
            dx_s(p, d).start()

    def tokens_middle(p, d):
        dx_s(p, d).wait_recv()
        for yy in range(4):
            part = dxf[p, d, rows((yy * 2 + co) * TB, TB)] + dxsr[p, d, yy].astype(F32)
            dxyf[p, d, yy] = part
            dxys[p, d, yy] = part.astype(BF16)
        for dy in (2, 1, 3):
            dx_y(p, d, dy).start()

    def tokens_sum(p, d):
        dx_y_all(p, d).wait_recv()
        value = dxyf[p, d, y]
        for i in range(3):
            value = value + dxyr[p, d, i].astype(F32)
        if p:
            dxcs[d] = value.astype(BF16)
            dx_c(d).start()
        else:
            dx_c(d).wait_recv()
            r_tok[:, cols(d)] = (value + dxcr[d].astype(F32)).astype(BF16)

    local = [pltpu.make_async_copy((tok, cot)[a], tslot(a, c, y, co), m_loc.at[a]) for a in range(2)]
    local += [pltpu.make_async_copy(wcols(c, j), wslot(j, c, x), m_loc.at[2 + j]) for j in range(NJ)]
    local += [pltpu.make_async_copy(wout, wo.at[rows(x * WB, WB)], m_loc.at[5])]
    results = ((r_tok, o_tok), (r_win, o_win), (r_wout, o_wout))
    result_tok, result_in, result_out = [pltpu.make_async_copy(*pair, m_res.at[i]) for i, pair in enumerate(results)]
    for copy in local:
        copy.start()
    barrier = pltpu.get_barrier_semaphore()
    partners = [dev(fs=1), dev(fc=1), dev(dk=1), dev(dk=3)]
    for d in (1, 2, 3):
        partners += [dev(dy=d), dev(dx=d)]
    for to in partners:
        pl.semaphore_signal(barrier, inc=1, device_id=to, device_id_type=MESH)
    pl.semaphore_wait(barrier, len(partners))

    wi_c(0).start()
    for d in (2, 1, 3):
        wi_x(0, 0, d).start()
        ag_y(0, 0, d).start()
    ag_c(0).start()
    ag_s(0, 0, 0).start()
    wi_c(1).start()
    wi_c(2).start()
    ag_c(1).start()
    wi_c(0).wait_recv()
    for d in (2, 1, 3):
        wi_x(0, 1, d).start()
    for r in range(2):
        wi_n(1, 0, r).start()
    ag_c(0).wait_recv()
    for d in (2, 1, 3):
        ag_y(0, 1, d).start()
    ag_s(0, 1, 0).start()
    for d in (1, 3, 2):
        ag_y(0, 0, d).wait_recv()
        ag_s(0, 0, d).start()
    wi_c(1).wait_recv()
    for r in range(2):
        wi_n(1, 1, r).start()
    for copy in local:
        copy.wait()
    ag_s_all(0, 0).wait_recv()
    wi_x_all(0).wait_recv()
    product(0)
    for p in range(2):
        m = cp(wslot(1, 0, 0), wslot(1, 0, 0), 1, m_wif.at[1, p], dev(dx=1))
        m.wait_recv()
        wi_f(1, p).start()
    wi_c(2).wait_recv()
    for p in range(2):
        for r in range(2):
            wi_n(2, p, r).start()
    for d in (1, 3, 2):
        ag_y(0, 1, d).wait_recv()
        ag_s(0, 1, d).start()
    for d in (2, 1, 3):
        ag_y(1, 0, d).start()
    ag_s(1, 0, 0).start()
    ag_c(1).wait_recv()
    for d in (2, 1, 3):
        ag_y(1, 1, d).start()
    ag_s(1, 1, 0).start()
    ag_s_all(0, 1).wait_recv()
    product(1)
    middle(0)
    for r in range(2):
        wo_n(r).start()

    for t in range(2, 2 * NU + 4):
        if t == 2:
            wi_x_all(1).wait_recv()
        if t == 3:
            for p in range(2):
                m = cp(wslot(2, 0, 0), wslot(2, 0, 0), 1, m_wif.at[2, p], dev(dx=1))
                m.wait_recv()
                wi_f(2, p).start()
        if t == 4:
            wi_x_all(2).wait_recv()
        if t == NU:
            wo_f_all().wait_recv()
            for p in (0, 1):
                ag_s_all(1, p).wait_recv()
        if t < 2 * NU:
            product(t)
        if t - 1 < 2 * NU:
            middle(t - 1)
        if t - 2 < 2 * NU:
            finish(t - 2)
        if 0 <= t - 3 < 2 * NU:
            forward(t - 3)
        if t == 4:
            for p in (0, 1):
                for d in (1, 3, 2):
                    ag_y(1, p, d).wait_recv()
                    ag_s(1, p, d).start()
        if t == NU - 1:
            for r in range(2):
                wo_n(r).wait_recv()
                wo_f(r).start()
        if t == NU + 3:
            for u in range(NU):
                arrived(u)
            weight_out_part()
        if t == NU + 5:
            weight_out_middle()
        u = t - 4
        if u >= NU:
            a, j, p = unit(u)
            arrived(u)
            if p:
                weight_in_half(j, 1)
                for d in range(ND):
                    tokens_part(1, j, d)
            elif j < NJ - 1:
                weight_in_part(j)
                for d in range(ND):
                    tokens_part(0, j, d)
                for d in range(ND):
                    (tokens_middle, tokens_sum)[j](1, d)
                if j == 1:
                    weight_in_middle(0)
    for d in range(ND):
        tokens_part(0, NJ - 1, d)
    weight_in_part(NJ - 1)
    weight_in_middle(1)
    for d in range(ND):
        tokens_middle(0, d)
    weight_out_finish()
    for j in range(NJ - 1):
        weight_in_sum(j, 1)
        weight_in_sum(j, 0)
    weight_in_sum(NJ - 1, 1)
    for d in range(ND):
        tokens_sum(0, d)
    result_tok.start()
    weight_in_sum(NJ - 1, 0)
    for j in range(NJ):
        weight_in_finish(j)
    result_in.start()

    whole = (
        tg.at[:, pl.ds(0, 15 * TB)], wi.at[:, pl.ds(0, 7 * WB)], wo.at[pl.ds(0, 3 * WB)], s1s, s2s,
        hg.at[:, :, pl.ds(0, 6 * OWN)], o1s, o2s, dwcs, dxss, dxyr, dxcs, i1s, i2s, dwis,
    )
    for family, ref in enumerate(whole):
        cp(ref, ref, family, m_agc.at[0], dev(fs=1)).wait_send()
    for copy in (result_tok, result_in, result_out):
        copy.wait()


def hand_over(*refs):
    sems = refs[6]
    copies = [pltpu.make_async_copy(refs[i], refs[3 + i], sems.at[i]) for i in range(3)]
    for copy in copies:
        copy.start()
    for copy in copies:
        copy.wait()


def shards(tokens, cotangent, weight_in, weight_out):
    scale = float(tokens.shape[0] * lax.axis_size("out") * lax.axis_size("dep")) ** (-0.5)
    vmem, dma = pltpu.VMEM, pltpu.SemaphoreType.DMA
    hbm = pl.BlockSpec(memory_space=pl.ANY)
    shapes = tuple(jax.ShapeDtypeStruct(a.shape, BF16) for a in (tokens, weight_in, weight_out))
    results = pl.pallas_call(
        functools.partial(kernel, scale),
        out_shape=shapes,
        in_specs=[hbm] * 4,
        out_specs=(hbm,) * 3,
        scratch_shapes=[
            vmem((2, TOK, WID), BF16),
            vmem((NJ, WID, CH), BF16),
            vmem((HID, WID), BF16),
            vmem((4, HALF, CH), F32),
            vmem((2 * NU, 2, 2, TB, CH), BF16),
            vmem((2 * NU, 2, 2, TB, CH), BF16),
            vmem((2 * NU, 2, TB, CH), BF16),
            vmem((2 * NU, 2, TB, CH), BF16),
            vmem((2, NJ, TOK, CH), BF16),
            vmem((NJ, 2, 2, TB, CH), F32),
            vmem((HID, WID), F32),
            vmem((2, 2, OWN, WID), BF16),
            vmem((2, 2, OWN, WID), BF16),
            vmem((2, OWN, WID), BF16),
            vmem((2, OWN, WID), BF16),
            vmem((NJ, WID, CH), F32),
            vmem((NJ - 1, 2, 2, WB, CH), BF16),
            vmem((NJ - 1, 2, 2, WB, CH), BF16),
            vmem((NJ - 1, 2, WB, CH), BF16),
            vmem((NJ - 1, 2, WB, CH), BF16),
            vmem((2, 3, WB, CH), BF16),
            vmem((2, 3, WB, CH), BF16),
            vmem((NJ, WB, CH), BF16),
            vmem((NJ, WB, CH), BF16),
            vmem((2, ND, HALF, DC), F32),
            vmem((2, ND, 4, TB, DC), BF16),
            vmem((2, ND, 4, TB, DC), BF16),
            vmem((2, ND, 4, TB, DC), F32),
            vmem((2, ND, 4, TB, DC), BF16),
            vmem((2, ND, 3, TB, DC), BF16),
            vmem((ND, TB, DC), BF16),
            vmem((ND, TB, DC), BF16),
            vmem((TB, WID), BF16),
            vmem((WB, WID), BF16),
            vmem((WB, WID), BF16),
            dma((6,)),
            dma((3,)),
            dma((15,)),
            dma((2,)),
            dma((2, 2, 3)),
            dma((2, 2)),
            dma((NJ,)),
            dma((NJ,)),
            dma((NJ, 2)),
            dma,
            dma((2,)),
            dma((2 * NU, 2)),
            dma((2 * NU, 2)),
            dma((2 * NU, 2)),
            dma((2 * NU, 2)),
            dma((2,)),
            dma((2,)),
            dma((NJ - 1, 2)),
            dma((NJ - 1, 2)),
            dma((2,)),
            dma((NJ,)),
            dma((2, ND)),
            dma((2, ND)),
            dma((ND,)),
        ],
        compiler_params=pltpu.CompilerParams(
            collective_id=0, has_side_effects=True, vmem_limit_bytes=61 * 2**20
        ),
        cost_estimate=pl.CostEstimate(flops=11 * 10**9, bytes_accessed=3 * 10**6, transcendentals=0),
    )(tokens, cotangent, weight_in, weight_out)
    return pl.pallas_call(
        hand_over, out_shape=shapes, in_specs=[hbm] * 3, out_specs=(hbm,) * 3, scratch_shapes=[dma((3,))]
    )(*results)


def solution(mesh):
    in_specs = (
        P(("dep", "out"), "inp"),
        P(("dep", "out"), "inp"),
        P(("inp", "dep"), "out"),
        P(("out", "dep"), "inp"),
    )
    out_specs = (P(("dep", "out"), "inp"), P(("inp", "dep"), "out"), P(("out", "dep"), "inp"))
    return jax.shard_map(shards, mesh=mesh, in_specs=in_specs, out_specs=out_specs, check_vma=False)
```

```python
import functools

import jax
import jax.numpy as jnp
from jax import lax
from jax.experimental import pallas as pl
from jax.experimental.pallas import tpu as pltpu
from jax.sharding import PartitionSpec as P

MESH = pl.DeviceIdType.MESH
BF16, F32 = jnp.bfloat16, jnp.float32
NJ, CH = 3, 256
NU = 2 * NJ
ORDER = ((0, 1), (0, 0), (1, 1), (1, 0), (2, 1), (2, 0))
ND, DC = 2, 768
OB, OH = 64, 32
STEP = (1, 3)
TB, WB = 48, 192
TOK, WID, HID = 768, 1536, 768
HALF, OWN = 384, 96


def dot(a, b, ca, cb):
    return lax.dot_general(a, b, (((ca,), (cb,)), ((), ())), preferred_element_type=F32)


def gelu_parts(preact):
    normal_cdf = 0.5 * (1.0 + lax.erf(preact * 0.7071067811865476))
    density = jnp.exp(-0.5 * preact * preact) * 0.3989422804014327
    return preact * normal_cdf, normal_cdf + preact * density


def kernel(
    scale, tok, cot, win, wout, o_tok, o_win, o_wout,
    tg, wl, wst, wi, wo, pf, s1s, s1r, s2s, s2r, hg, slope, dwof, o1s, o1r, o2s, o2r,
    dwif, i1s, i1r, i2s, i2r, dwis, dwir, dwcs, dwcr, dxf, dxss, dxsr, dxyf, dxys, dxyr, dxcs, dxcr,
    r_tok, r_win, r_wout, m_loc, m_res, sent, m_agc, m_agy, m_ags, m_wic, m_wix, m_wif, m_wox, m_wof, m_s1, m_s2, m_h1, m_h2,
    m_o1, m_o2, m_i1, m_i2, m_dwi, m_dwc, m_dxs, m_dxy, m_dxc,
):
    k, out, dep = lax.axis_index("inp"), lax.axis_index("out"), lax.axis_index("dep")
    y, co, c, x = out // 2, out % 2, dep // 4, dep % 4
    oc, oco = 1 - c, 1 - co
    half = (c, oc)

    def dev(dk=0, dy=0, dx=0, fc=0, fs=0):
        o = (y + dy) % 4 * 2 + (oco if fs else co)
        d = (oc if fc else c) * 4 + (x + dx) % 4
        return {"inp": (k + dk) % 4, "out": o, "dep": d}

    def cp(src, dst, family, recv, to):
        return pltpu.make_async_remote_copy(
            src_ref=src, dst_ref=dst, send_sem=sent.at[family], recv_sem=recv, device_id=to, device_id_type=MESH
        )

    def rows(start, n):
        return pl.ds(pl.multiple_of(start, 16), n)

    def tslot(a, cc, yy, oo):
        return tg.at[a, rows(((cc * 4 + yy) * 2 + oo) * TB, TB)]

    def ag_c(a):
        return cp((tok, cot)[a], tslot(a, c, y, co), 0, m_agc.at[a], dev(fc=1))

    def ag_y(a, p, dy):
        slot = tslot(a, half[p], y, co)
        return cp(slot if p else (tok, cot)[a], slot, 0, m_agy.at[a, p, dy - 1], dev(dy=dy))

    def ag_s(a, p, dy):
        slot = tslot(a, half[p], (y + 4 - dy) % 4, co)
        src = (tok, cot)[a] if (p == 0 and dy == 0) else slot
        return cp(src, slot, 0, m_ags.at[a, p], dev(fs=1))

    def ag_s_all(a, p):
        ref = tg.at[a, pl.ds(0, 4 * TB)]
        return cp(ref, ref, 0, m_ags.at[a, p], dev(fs=1))

    def wslot(j, cc, xx):
        return wi.at[j, rows((cc * 4 + xx) * WB, WB)]

    def wi_c(j):
        return cp(wst.at[oc, j], wslot(j, c, x), 1, m_wic.at[j], dev(fc=1))

    def wi_x(j, p, dx):
        slot = wslot(j, half[p], x)
        return cp(slot if p else wst.at[c, j], slot, 1, m_wix.at[j], dev(dx=dx))

    def wi_x_all(j):
        ref = wi.at[j, pl.ds(0, (4 if j else 6) * WB)]
        return cp(ref, ref, 1, m_wix.at[j], dev(dx=1))

    def wi_n(j, p, r):
        slot = wslot(j, half[p], x)
        sem = m_wif.at[j, p] if p == r else m_wix.at[j]
        return cp(slot if p else wst.at[c, j], slot, 1, sem, dev(dx=STEP[r]))

    def wi_f(j, p):
        slot = wslot(j, half[p], (x + STEP[1 - p]) % 4)
        return cp(slot, slot, 1, m_wix.at[j], dev(dx=STEP[p]))

    def wi_pass_on(j):
        slot = wslot(j, 0, 0)
        for p in range(2):
            cp(slot, slot, 1, m_wif.at[j, p], dev(dx=1)).wait_recv()
            wi_f(j, p).start()

    def wo_part(j, xx, part):
        return wo.at[j, rows(xx % 4 * OB + part * OH, OH)]

    def wo_n(j, r, part):
        sem = m_wof.at[j, r] if part == r else m_wox.at[j]
        src = wout.at[pl.ds(j * OB + part * OH, OH)]
        return cp(src, wo_part(j, x, part), 2, sem, dev(dx=STEP[r]))

    def wo_f(j, r):
        slot = wo_part(j, x + STEP[1 - r], r)
        return cp(slot, slot, 2, m_wox.at[j], dev(dx=STEP[r]))

    def wo_all(j):
        ref = wo.at[j, pl.ds(0, 4 * OH)]
        return cp(ref, ref, 2, m_wox.at[j], dev(dx=1))

    def wo_send(j):
        for i in range(2):
            for r in range(2):
                wo_n(j, r, (r + i) % 2).start()

    def wo_pass_on(j):
        for r in range(2):
            wo_n(j, r, r).wait_recv()
            wo_f(j, r).start()

    def unit(u):
        a, i = divmod(u, NU)
        return (a, *ORDER[i]) if a else (a, i // 2, i % 2)

    def s1(u, r):
        return cp(s1s.at[u, r], s1r.at[u, r], 3, m_s1.at[u, r], dev(dk=STEP[r]))

    def s2(u, r):
        return cp(s2s.at[u, r], s2r.at[u, r], 4, m_s2.at[u, r], dev(dk=STEP[r]))

    def hrows(u, owner, part, n):
        a, j, p = unit(u)
        return hg.at[a, j, rows(half[p] * HALF + owner % 4 * OWN + part * TB, n)]

    def h1(u, r):
        slot = hrows(u, k, 0, OWN)
        return cp(slot, slot, 5, m_h1.at[u, r], dev(dk=STEP[r]))

    def h2(u, r):
        slot = hrows(u, k + STEP[1 - r], r, TB)
        return cp(slot, slot, 5, m_h2.at[u, r], dev(dk=STEP[r]))

    def o1(j, r):
        return cp(o1s.at[j, r], o1r.at[j, r], 6, m_o1.at[j, r], dev(dx=STEP[r]))

    def o2(j, r):
        return cp(o2s.at[j, r], o2r.at[j, r], 7, m_o2.at[j, r], dev(dx=STEP[r]))

    def i1(j, r):
        return cp(i1s.at[j, r], i1r.at[j, r], 12, m_i1.at[j, r], dev(dx=STEP[r]))

    def i2(j, r):
        return cp(i2s.at[j, r], i2r.at[j, r], 13, m_i2.at[j, r], dev(dx=STEP[r]))

    def dwi_x(p, dx):
        return cp(dwis.at[p, dx - 1], dwir.at[p, dx - 1], 14, m_dwi.at[p], dev(dx=dx))

    def dwi_x_all(p):
        return cp(dwir.at[p], dwir.at[p], 14, m_dwi.at[p], dev(dx=1))

    def dw_c(j):
        return cp(dwcs.at[j], dwcr.at[j], 8, m_dwc.at[j], dev(fc=1))

    def dx_s(p, d):
        return cp(dxss.at[p, d], dxsr.at[p, d], 9, m_dxs.at[p, d], dev(fs=1))

    def dx_y(p, d, dy):
        return cp(dxys.at[p, d, (y + dy) % 4], dxyr.at[p, d, dy - 1], 10, m_dxy.at[p, d], dev(dy=dy))

    def dx_y_all(p, d):
        return cp(dxyr.at[p, d], dxyr.at[p, d], 10, m_dxy.at[p, d], dev(dy=1))

    def dx_c(d):
        return cp(dxcs.at[d], dxcr.at[d], 11, m_dxc.at[d], dev(fc=1))

    def product(u):
        a, j, p = unit(u)
        lhs = tg[a, rows(half[p] * HALF, HALF)]
        pf[u % 4] = dot(lhs, wo[j], 1, 1) if a else dot(lhs, wi[j], 1, 0)

        def piece(owner, part):
            return pf[u % 4, rows(owner % 4 * OWN + part * TB, TB)].astype(BF16)

        s1s[u, 0, 0] = piece(k + 2, 0)
        s1s[u, 0, 1] = piece(k + 1, 1)
        s1(u, 0).start()
        s1s[u, 1, 0] = piece(k + 2, 1)
        s1s[u, 1, 1] = piece(k + 3, 0)
        s1(u, 1).start()

    def middle(u):
        for r in range(2):
            s1(u, r).wait_recv()
            own = pf[u % 4, rows((k + STEP[r]) % 4 * OWN + r * TB, TB)]
            s2s[u, r] = (own + s1r[u, r, 0].astype(F32)).astype(BF16)
            s2(u, r).start()

    def finish(u):
        a, j, p = unit(u)
        for r in range(2):
            s2(u, r).wait_recv()
            value = pf[u % 4, rows(k * OWN + r * TB, TB)] + s2r[u, r].astype(F32) + s1r[u, 1 - r, 1].astype(F32)
            if a:
                value = value * slope[j, p, r]
            else:
                value, slope[j, p, r] = gelu_parts(value)
            hg[a, j, rows(half[p] * HALF + k * OWN + r * TB, TB)] = value.astype(BF16)
        for r in range(2):
            h1(u, r).start()

    def forward(u):
        for r in range(2):
            h1(u, r).wait_recv()
            h2(u, r).start()

    def arrived(u):
        for r in range(2):
            h2(u, r).wait_recv()

    def weight_out_part(j):
        dwof[j] = scale * dot(hg[0, j], tg[1], 0, 0)

        def piece(owner, part):
            return dwof[j, rows(owner % 4 * OB + part * OH, OH)].astype(BF16)

        for r in range(2):
            o1s[j, r, 0] = piece(x + 2, r)
            o1s[j, r, 1] = piece(x + STEP[r], 1 - r)
            o1(j, r).start()

    def weight_out_middle(j):
        for r in range(2):
            o1(j, r).wait_recv()
            own = dwof[j, rows((x + STEP[r]) % 4 * OB + r * OH, OH)]
            o2s[j, r] = (own + o1r[j, r, 0].astype(F32)).astype(BF16)
            o2(j, r).start()

    def weight_out_finish(j):
        for r in range(2):
            o2(j, r).wait_recv()
            value = dwof[j, rows(x * OB + r * OH, OH)] + o2r[j, r].astype(F32) + o1r[j, 1 - r, 1].astype(F32)
            r_wout[pl.ds(j * OB + r * OH, OH)] = value.astype(BF16)

    def weight_in_half(j, p):
        value = scale * dot(tg[0, rows(half[p] * HALF, HALF)], hg[1, j, rows(half[p] * HALF, HALF)], 0, 0)
        if p:
            dwif[j] = value
        else:
            dwif[j] += value

    def weight_in_piece(j, p, owner):
        return dwif[j, rows((half[p] * 4 + owner % 4) * WB, WB)]

    def weight_in_part(j):
        weight_in_half(j, 0)
        if j == NJ - 1:
            for p in (1, 0):
                for d in (2, 1, 3):
                    dwis[p, d - 1] = weight_in_piece(j, p, x + d).astype(BF16)
                    dwi_x(p, d).start()
        else:
            for r in range(2):
                i1s[j, r, 0] = weight_in_piece(j, 1 - r, x + 2).astype(BF16)
                i1s[j, r, 1] = weight_in_piece(j, r, x + STEP[r]).astype(BF16)
                i1(j, r).start()

    def weight_in_middle(j):
        for r in range(2):
            i1(j, r).wait_recv()
            i2s[j, r] = (weight_in_piece(j, 1 - r, x + STEP[r]) + i1r[j, r, 0].astype(F32)).astype(BF16)
            i2(j, r).start()

    def weight_in_result(cc, j, value):
        for xx in range(4):
            r_win[cc, :, pl.ds(xx * WB + j * OB, OB)] = value[:, xx * OB : (xx + 1) * OB]

    def weight_in_sum(j, p):
        value = weight_in_piece(j, p, x)
        if j == NJ - 1:
            dwi_x_all(p).wait_recv()
            for d in range(3):
                value = value + dwir[p, d].astype(F32)
        else:
            i2(j, 1 - p).wait_recv()
            value = value + i2r[j, 1 - p].astype(F32) + i1r[j, p, 1].astype(F32)
        if p:
            dwcs[j] = value.astype(BF16)
            dw_c(j).start()
        else:
            weight_in_result(c, j, value.astype(BF16))

    def weight_in_finish(j):
        dw_c(j).wait_recv()
        weight_in_result(oc, j, dwcr[j])

    def cols(d):
        return pl.ds(d * DC, DC)

    def tokens_part(p, j, d):
        part = dot(hg[1, j, rows(half[p] * HALF, HALF)], wi[j, cols(d)], 1, 1)
        if j == 0:
            dxf[p, d] = part
        else:
            dxf[p, d] += part
        if j == NJ - 1:
            for yy in range(4):
                dxss[p, d, yy] = dxf[p, d, rows((yy * 2 + oco) * TB, TB)].astype(BF16)
            dx_s(p, d).start()

    def tokens_middle(p, d):
        dx_s(p, d).wait_recv()
        for yy in range(4):
            part = dxf[p, d, rows((yy * 2 + co) * TB, TB)] + dxsr[p, d, yy].astype(F32)
            dxyf[p, d, yy] = part
            dxys[p, d, yy] = part.astype(BF16)
        for dy in (2, 1, 3):
            dx_y(p, d, dy).start()

    def tokens_sum(p, d):
        dx_y_all(p, d).wait_recv()
        value = dxyf[p, d, y]
        for i in range(3):
            value = value + dxyr[p, d, i].astype(F32)
        if p:
            dxcs[d] = value.astype(BF16)
            dx_c(d).start()
        else:
            dx_c(d).wait_recv()
            r_tok[:, cols(d)] = (value + dxcr[d].astype(F32)).astype(BF16)

    local = [pltpu.make_async_copy((tok, cot)[a], tslot(a, c, y, co), m_loc.at[a]) for a in range(2)]
    local += [pltpu.make_async_copy(wout.at[pl.ds(j * OB, OB)], wo.at[j, rows(x * OB, OB)], m_loc.at[2 + j]) for j in range(NJ)]
    columns = pltpu.make_async_copy(win, wl, m_loc.at[5])
    result_tok = pltpu.make_async_copy(r_tok, o_tok, m_res.at[0])
    result_out = pltpu.make_async_copy(r_wout, o_wout, m_res.at[1])
    result_in = [pltpu.make_async_copy(r_win.at[i], o_win.at[:, pl.ds(i * HID, HID)], m_res.at[2 + i]) for i in range(2)]
    columns.start()
    for copy in local:
        copy.start()
    barrier = pltpu.get_barrier_semaphore()
    partners = [dev(fs=1), dev(fc=1), dev(dk=1), dev(dk=3)]
    for d in (1, 2, 3):
        partners += [dev(dy=d), dev(dx=d)]
    for to in partners:
        pl.semaphore_signal(barrier, inc=1, device_id=to, device_id_type=MESH)
    columns.wait()
    for j in range(NJ):
        for cc in range(2):
            for xx in range(4):
                wst[cc, j, :, pl.ds(xx * OB, OB)] = wl[:, pl.ds(cc * HID + xx * WB + j * OB, OB)]
        wi[j, rows((c * 4 + x) * WB, WB)] = wst[c, j]
    pl.semaphore_wait(barrier, len(partners))

    wi_c(0).start()
    for d in (2, 1, 3):
        wi_x(0, 0, d).start()
        ag_y(0, 0, d).start()
    ag_c(0).start()
    ag_s(0, 0, 0).start()
    wi_c(1).start()
    wi_c(2).start()
    ag_c(1).start()
    wi_c(0).wait_recv()
    for d in (2, 1, 3):
        wi_x(0, 1, d).start()
    for r in range(2):
        wi_n(1, 0, r).start()
    ag_c(0).wait_recv()
    for d in (2, 1, 3):
        ag_y(0, 1, d).start()
    ag_s(0, 1, 0).start()
    for d in (1, 3, 2):
        ag_y(0, 0, d).wait_recv()
        ag_s(0, 0, d).start()
    wi_c(1).wait_recv()
    for r in range(2):
        wi_n(1, 1, r).start()
    for r in range(2):
        wi_n(2, 0, r).start()
    for copy in local:
        copy.wait()
    ag_s_all(0, 0).wait_recv()
    wi_x_all(0).wait_recv()
    product(0)
    wi_c(2).wait_recv()
    for r in range(2):
        wi_n(2, 1, r).start()
    for d in (1, 3, 2):
        ag_y(0, 1, d).wait_recv()
        ag_s(0, 1, d).start()
    wi_pass_on(1)
    for d in (2, 1, 3):
        ag_y(1, 0, d).start()
    ag_s(1, 0, 0).start()
    ag_c(1).wait_recv()
    for d in (2, 1, 3):
        ag_y(1, 1, d).start()
    ag_s(1, 1, 0).start()
    ag_s_all(0, 1).wait_recv()
    product(1)

    for t in range(1, 2 * NU + 4):
        if t - 1 < 2 * NU:
            middle(t - 1)
        if 0 <= t - 2 < 2 * NU:
            finish(t - 2)
        if 0 <= t - 3 < 2 * NU:
            forward(t - 3)
        if t == 1:
            wi_x_all(1).wait_recv()
        if t == 3:
            wi_x_all(2).wait_recv()
        if t == NU - 1:
            for p in (0, 1):
                ag_s_all(1, p).wait_recv()
        if t >= NU - 1 and (t + 1 - NU) % 2 == 0 and t + 1 < 2 * NU:
            wo_all((t + 1 - NU) // 2).wait_recv()
        if t + 1 < 2 * NU:
            product(t + 1)
        if t == 1:
            wo_send(0)
        if t == 2:
            wi_pass_on(2)
            wo_send(1)
        if t == 3:
            for p in (0, 1):
                for d in (1, 3, 2):
                    ag_y(1, p, d).wait_recv()
                    ag_s(1, p, d).start()
            wo_pass_on(0)
            wo_send(2)
        if t in (4, 5):
            wo_pass_on(t - 3)
        for j in range(NJ):
            if t == 2 * j + 5:
                arrived(2 * j)
                arrived(2 * j + 1)
                weight_out_part(j)
            if t == 2 * j + 6:
                weight_out_middle(j)
            if t == 2 * j + 8:
                weight_out_finish(j)
        if t == 2 * NU:
            result_out.start()
        u = t - 4
        if u == NU + 5:
            for d in range(ND):
                tokens_middle(1, d)
        if u >= NU:
            a, j, p = unit(u)
            arrived(u)
            if p:
                weight_in_half(j, 1)
            for d in range(ND):
                tokens_part(p, j, d)
            if not p:
                weight_in_part(j)
            if u == NU + 2:
                weight_in_middle(0)
    for d in range(ND):
        tokens_middle(0, d)
    weight_in_middle(1)
    for p in (1, 0):
        weight_in_sum(0, p)
    for d in range(ND):
        tokens_sum(1, d)
    weight_in_sum(2, 1)
    for p in (1, 0):
        weight_in_sum(1, p)
    for d in range(ND):
        tokens_sum(0, d)
    result_tok.start()
    weight_in_sum(2, 0)
    for j in range(NJ):
        weight_in_finish(j)
    for copy in result_in:
        copy.start()

    whole = (
        tg.at[:, pl.ds(0, 15 * TB)], wi.at[:, pl.ds(0, 7 * WB)], wo.at[:, pl.ds(0, 3 * OB)], s1s, s2s,
        hg.at[:, :, pl.ds(0, 6 * OWN)], o1s, o2s, dwcs, dxss, dxyr, dxcs, i1s, i2s, dwis,
    )
    for family, ref in enumerate(whole):
        cp(ref, ref, family, m_agc.at[0], dev(fs=1)).wait_send()
    for copy in (result_tok, result_out, *result_in):
        copy.wait()


def hand_over(*refs):
    sems = refs[9]
    loads = [pltpu.make_async_copy(refs[i], refs[6 + i], sems.at[i]) for i in range(3)]
    stores = [pltpu.make_async_copy(refs[6 + i], refs[3 + i], sems.at[3 + i]) for i in range(3)]
    for copy in loads:
        copy.start()
    for load, store in zip(loads, stores):
        load.wait()
        store.start()
    for copy in stores:
        copy.wait()


def shards(tokens, cotangent, weight_in, weight_out):
    scale = float(tokens.shape[0] * lax.axis_size("out") * lax.axis_size("dep")) ** (-0.5)
    vmem, dma = pltpu.VMEM, pltpu.SemaphoreType.DMA
    hbm = pl.BlockSpec(memory_space=pl.ANY)
    shapes = tuple(jax.ShapeDtypeStruct(a.shape, BF16) for a in (tokens, weight_in, weight_out))
    results = pl.pallas_call(
        functools.partial(kernel, scale),
        out_shape=shapes,
        in_specs=[hbm] * 4,
        out_specs=(hbm,) * 3,
        scratch_shapes=[
            vmem((2, TOK, WID), BF16),
            vmem((WB, 2 * HID), BF16),
            vmem((2, NJ, WB, CH), BF16),
            vmem((NJ, WID, CH), BF16),
            vmem((NJ, CH, WID), BF16),
            vmem((4, HALF, CH), F32),
            vmem((2 * NU, 2, 2, TB, CH), BF16),
            vmem((2 * NU, 2, 2, TB, CH), BF16),
            vmem((2 * NU, 2, TB, CH), BF16),
            vmem((2 * NU, 2, TB, CH), BF16),
            vmem((2, NJ, TOK, CH), BF16),
            vmem((NJ, 2, 2, TB, CH), F32),
            vmem((NJ, CH, WID), F32),
            vmem((NJ, 2, 2, OH, WID), BF16),
            vmem((NJ, 2, 2, OH, WID), BF16),
            vmem((NJ, 2, OH, WID), BF16),
            vmem((NJ, 2, OH, WID), BF16),
            vmem((NJ, WID, CH), F32),
            vmem((NJ - 1, 2, 2, WB, CH), BF16),
            vmem((NJ - 1, 2, 2, WB, CH), BF16),
            vmem((NJ - 1, 2, WB, CH), BF16),
            vmem((NJ - 1, 2, WB, CH), BF16),
            vmem((2, 3, WB, CH), BF16),
            vmem((2, 3, WB, CH), BF16),
            vmem((NJ, WB, CH), BF16),
            vmem((NJ, WB, CH), BF16),
            vmem((2, ND, HALF, DC), F32),
            vmem((2, ND, 4, TB, DC), BF16),
            vmem((2, ND, 4, TB, DC), BF16),
            vmem((2, ND, 4, TB, DC), F32),
            vmem((2, ND, 4, TB, DC), BF16),
            vmem((2, ND, 3, TB, DC), BF16),
            vmem((ND, TB, DC), BF16),
            vmem((ND, TB, DC), BF16),
            vmem((TB, WID), BF16),
            vmem((2, WB, HID), BF16),
            vmem((WB, WID), BF16),
            dma((6,)),
            dma((4,)),
            dma((15,)),
            dma((2,)),
            dma((2, 2, 3)),
            dma((2, 2)),
            dma((NJ,)),
            dma((NJ,)),
            dma((NJ, 2)),
            dma((NJ,)),
            dma((NJ, 2)),
            dma((2 * NU, 2)),
            dma((2 * NU, 2)),
            dma((2 * NU, 2)),
            dma((2 * NU, 2)),
            dma((NJ, 2)),
            dma((NJ, 2)),
            dma((NJ - 1, 2)),
            dma((NJ - 1, 2)),
            dma((2,)),
            dma((NJ,)),
            dma((2, ND)),
            dma((2, ND)),
            dma((ND,)),
        ],
        compiler_params=pltpu.CompilerParams(
            collective_id=0, has_side_effects=True, vmem_limit_bytes=61 * 2**20
        ),
        cost_estimate=pl.CostEstimate(flops=11 * 10**9, bytes_accessed=3 * 10**6, transcendentals=0),
    )(tokens, cotangent, weight_in, weight_out)
    return pl.pallas_call(
        hand_over,
        out_shape=shapes,
        in_specs=[hbm] * 3,
        out_specs=(hbm,) * 3,
        scratch_shapes=[vmem(a.shape, BF16) for a in shapes] + [dma((6,))],
    )(*results)


def solution(mesh):
    in_specs = (
        P(("dep", "out"), "inp"),
        P(("dep", "out"), "inp"),
        P(("inp", "dep"), "out"),
        P(("out", "dep"), "inp"),
    )
    out_specs = (P(("dep", "out"), "inp"), P(("inp", "dep"), "out"), P(("out", "dep"), "inp"))
    return jax.shard_map(shards, mesh=mesh, in_specs=in_specs, out_specs=out_specs, check_vma=False)
```

```python
import functools

import jax
import jax.numpy as jnp
from jax import lax
from jax.experimental import pallas as pl
from jax.experimental.pallas import tpu as pltpu
from jax.sharding import PartitionSpec as P

MESH = pl.DeviceIdType.MESH
BF16, F32 = jnp.bfloat16, jnp.float32
NJ, CH = 3, 256
NU = 2 * NJ
ORDER = ((0, 1), (0, 0), (1, 1), (2, 1), (1, 0), (2, 0))
ND, DC = 3, 512
OB, OH = 64, 32
STEP = (1, 3)
TB, WB = 48, 192
TOK, WID, HID = 768, 1536, 768
HALF, OWN = 384, 96


def dot(a, b, ca, cb):
    return lax.dot_general(a, b, (((ca,), (cb,)), ((), ())), preferred_element_type=F32)


def gelu_parts(preact):
    normal_cdf = 0.5 * (1.0 + lax.erf(preact * 0.7071067811865476))
    density = jnp.exp(-0.5 * preact * preact) * 0.3989422804014327
    return preact * normal_cdf, normal_cdf + preact * density


def kernel(
    scale, tok, cot, win, wout, r_tok, o_win, r_wout,
    tg, wl, wst, wi, wo, pf, s1s, s1r, s2s, s2r, hg, slope, dwof, o1s, o1r, o2s, o2r,
    dwif, dwis, dwir, dwcs, dwcr, dxf, dxss, dxsr, dxyf, dxys, dxyr, dxcs, dxcr,
    r_win, m_loc, m_res, sent, m_agc, m_agy, m_ags, m_wic, m_wix, m_wif, m_wox, m_wof, m_s1, m_s2, m_h1, m_h2,
    m_o1, m_o2, m_dwi, m_dwc, m_dxs, m_dxy, m_dxc,
):
    k, out, dep = lax.axis_index("inp"), lax.axis_index("out"), lax.axis_index("dep")
    y, co, c, x = out // 2, out % 2, dep // 4, dep % 4
    oc, oco = 1 - c, 1 - co
    half = (c, oc)

    def dev(dk=0, dy=0, dx=0, fc=0, fs=0):
        o = (y + dy) % 4 * 2 + (oco if fs else co)
        d = (oc if fc else c) * 4 + (x + dx) % 4
        return {"inp": (k + dk) % 4, "out": o, "dep": d}

    def cp(src, dst, family, recv, to):
        return pltpu.make_async_remote_copy(
            src_ref=src, dst_ref=dst, send_sem=sent.at[family], recv_sem=recv, device_id=to, device_id_type=MESH
        )

    def rows(start, n):
        return pl.ds(pl.multiple_of(start, 16), n)

    def tslot(a, cc, yy, oo):
        return tg.at[a, rows(((cc * 4 + yy) * 2 + oo) * TB, TB)]

    def ag_c(a):
        return cp((tok, cot)[a], tslot(a, c, y, co), 0, m_agc.at[a], dev(fc=1))

    def ag_y(a, p, dy):
        slot = tslot(a, half[p], y, co)
        return cp(slot if p else (tok, cot)[a], slot, 0, m_agy.at[a, p, dy - 1], dev(dy=dy))

    def ag_s(a, p, dy):
        slot = tslot(a, half[p], (y + 4 - dy) % 4, co)
        src = (tok, cot)[a] if (p == 0 and dy == 0) else slot
        return cp(src, slot, 0, m_ags.at[a, p], dev(fs=1))

    def ag_s_all(a, p):
        ref = tg.at[a, pl.ds(0, 4 * TB)]
        return cp(ref, ref, 0, m_ags.at[a, p], dev(fs=1))

    def wslot(j, cc, xx):
        return wi.at[j, rows((cc * 4 + xx) * WB, WB)]

    def wi_c(j):
        return cp(wst.at[oc, j], wslot(j, c, x), 1, m_wic.at[j], dev(fc=1))

    def wi_x(j, p, dx):
        slot = wslot(j, half[p], x)
        return cp(slot if p else wst.at[c, j], slot, 1, m_wix.at[j], dev(dx=dx))

    def wi_x_all(j):
        ref = wi.at[j, pl.ds(0, (4 if j else 6) * WB)]
        return cp(ref, ref, 1, m_wix.at[j], dev(dx=1))

    def wi_n(j, p, r):
        slot = wslot(j, half[p], x)
        sem = m_wif.at[j, p] if p == r else m_wix.at[j]
        return cp(slot if p else wst.at[c, j], slot, 1, sem, dev(dx=STEP[r]))

    def wi_f(j, p):
        slot = wslot(j, half[p], (x + STEP[1 - p]) % 4)
        return cp(slot, slot, 1, m_wix.at[j], dev(dx=STEP[p]))

    def wi_pass_on(j):
        slot = wslot(j, 0, 0)
        for p in range(2):
            cp(slot, slot, 1, m_wif.at[j, p], dev(dx=1)).wait_recv()
            wi_f(j, p).start()

    def wo_part(j, xx, part):
        return wo.at[j, rows(xx % 4 * OB + part * OH, OH)]

    def wo_n(j, r, part):
        sem = m_wof.at[j, r] if part == r else m_wox.at[j]
        src = wout.at[pl.ds(j * OB + part * OH, OH)]
        return cp(src, wo_part(j, x, part), 2, sem, dev(dx=STEP[r]))

    def wo_f(j, r):
        slot = wo_part(j, x + STEP[1 - r], r)
        return cp(slot, slot, 2, m_wox.at[j], dev(dx=STEP[r]))

    def wo_all(j):
        ref = wo.at[j, pl.ds(0, 4 * OH)]
        return cp(ref, ref, 2, m_wox.at[j], dev(dx=1))

    def wo_send(j):
        for i in range(2):
            for r in range(2):
                wo_n(j, r, (r + i) % 2).start()

    def wo_pass_on(j):
        for r in range(2):
            wo_n(j, r, r).wait_recv()
            wo_f(j, r).start()

    def unit(u):
        a, i = divmod(u, NU)
        return (a, *ORDER[i]) if a else (a, i // 2, i % 2)

    def s1(u, r):
        return cp(s1s.at[u, r], s1r.at[u, r], 3, m_s1.at[u, r], dev(dk=STEP[r]))

    def s2(u, r):
        return cp(s2s.at[u, r], s2r.at[u, r], 4, m_s2.at[u, r], dev(dk=STEP[r]))

    def hrows(u, owner, part, n):
        a, j, p = unit(u)
        return hg.at[a, j, rows(half[p] * HALF + owner % 4 * OWN + part * TB, n)]

    def h1(u, r):
        slot = hrows(u, k, 0, OWN)
        return cp(slot, slot, 5, m_h1.at[u, r], dev(dk=STEP[r]))

    def h2(u, r):
        slot = hrows(u, k + STEP[1 - r], r, TB)
        return cp(slot, slot, 5, m_h2.at[u, r], dev(dk=STEP[r]))

    def o1(j, r):
        return cp(o1s.at[j, r], o1r.at[j, r], 6, m_o1.at[j, r], dev(dx=STEP[r]))

    def o2(j, r):
        return cp(o2s.at[j, r], o2r.at[j, r], 7, m_o2.at[j, r], dev(dx=STEP[r]))

    def dwi_x(j, p, dx):
        return cp(dwis.at[j, p, dx - 1], dwir.at[j, p, dx - 1], 12, m_dwi.at[j, p], dev(dx=dx))

    def dwi_x_all(j, p):
        return cp(dwir.at[j, p], dwir.at[j, p], 12, m_dwi.at[j, p], dev(dx=1))

    def dw_c(j):
        return cp(dwcs.at[j], dwcr.at[j], 8, m_dwc.at[j], dev(fc=1))

    def dx_s(p, d):
        return cp(dxss.at[p, d], dxsr.at[p, d], 9, m_dxs.at[p, d], dev(fs=1))

    def dx_y(p, d, dy):
        return cp(dxys.at[p, d, (y + dy) % 4], dxyr.at[p, d, dy - 1], 10, m_dxy.at[p, d], dev(dy=dy))

    def dx_y_all(p, d):
        return cp(dxyr.at[p, d], dxyr.at[p, d], 10, m_dxy.at[p, d], dev(dy=1))

    def dx_c(d):
        return cp(dxcs.at[d], dxcr.at[d], 11, m_dxc.at[d], dev(fc=1))

    def product(u):
        a, j, p = unit(u)
        lhs = tg[a, rows(half[p] * HALF, HALF)]
        pf[u % 4] = dot(lhs, wo[j], 1, 1) if a else dot(lhs, wi[j], 1, 0)

        def piece(owner, part):
            return pf[u % 4, rows(owner % 4 * OWN + part * TB, TB)].astype(BF16)

        s1s[u, 0, 0] = piece(k + 2, 0)
        s1s[u, 0, 1] = piece(k + 1, 1)
        s1(u, 0).start()
        s1s[u, 1, 0] = piece(k + 2, 1)
        s1s[u, 1, 1] = piece(k + 3, 0)
        s1(u, 1).start()

    def middle(u):
        for r in range(2):
            s1(u, r).wait_recv()
            own = pf[u % 4, rows((k + STEP[r]) % 4 * OWN + r * TB, TB)]
            s2s[u, r] = (own + s1r[u, r, 0].astype(F32)).astype(BF16)
            s2(u, r).start()

    def finish(u):
        a, j, p = unit(u)
        for r in range(2):
            s2(u, r).wait_recv()
            value = pf[u % 4, rows(k * OWN + r * TB, TB)] + s2r[u, r].astype(F32) + s1r[u, 1 - r, 1].astype(F32)
            if a:
                value = value * slope[j, p, r]
            else:
                value, slope[j, p, r] = gelu_parts(value)
            hg[a, j, rows(half[p] * HALF + k * OWN + r * TB, TB)] = value.astype(BF16)
        for r in range(2):
            h1(u, r).start()

    def forward(u):
        for r in range(2):
            h1(u, r).wait_recv()
            h2(u, r).start()

    def arrived(u):
        for r in range(2):
            h2(u, r).wait_recv()

    def weight_out_part(j):
        dwof[j] = scale * dot(hg[0, j], tg[1], 0, 0)

        def piece(owner, part):
            return dwof[j, rows(owner % 4 * OB + part * OH, OH)].astype(BF16)

        for r in range(2):
            o1s[j, r, 0] = piece(x + 2, r)
            o1s[j, r, 1] = piece(x + STEP[r], 1 - r)
            o1(j, r).start()

    def weight_out_middle(j):
        for r in range(2):
            o1(j, r).wait_recv()
            own = dwof[j, rows((x + STEP[r]) % 4 * OB + r * OH, OH)]
            o2s[j, r] = (own + o1r[j, r, 0].astype(F32)).astype(BF16)
            o2(j, r).start()

    def weight_out_finish(j):
        for r in range(2):
            o2(j, r).wait_recv()
            value = dwof[j, rows(x * OB + r * OH, OH)] + o2r[j, r].astype(F32) + o1r[j, 1 - r, 1].astype(F32)
            r_wout[pl.ds(j * OB + r * OH, OH)] = value.astype(BF16)

    def weight_in_half(j, p):
        value = scale * dot(tg[0, rows(half[p] * HALF, HALF)], hg[1, j, rows(half[p] * HALF, HALF)], 0, 0)
        if p:
            dwif[j] = value
        else:
            dwif[j] += value

    def weight_in_piece(j, p, owner):
        return dwif[j, rows((half[p] * 4 + owner % 4) * WB, WB)]

    def weight_in_part(j):
        weight_in_half(j, 0)
        for p in (1, 0):
            for d in (2, 1, 3):
                dwis[j, p, d - 1] = weight_in_piece(j, p, x + d).astype(BF16)
                dwi_x(j, p, d).start()

    def weight_in_result(cc, j, value):
        for xx in range(4):
            r_win[cc, :, pl.ds(xx * WB + j * OB, OB)] = value[:, xx * OB : (xx + 1) * OB]

    def weight_in_sum(j, p):
        value = weight_in_piece(j, p, x)
        dwi_x_all(j, p).wait_recv()
        for d in range(3):
            value = value + dwir[j, p, d].astype(F32)
        if p:
            dwcs[j] = value.astype(BF16)
            dw_c(j).start()
        else:
            weight_in_result(c, j, value.astype(BF16))

    def weight_in_finish(j):
        dw_c(j).wait_recv()
        weight_in_result(oc, j, dwcr[j])

    def cols(d):
        return pl.ds(d * DC, DC)

    def tokens_part(p, j, d):
        part = dot(hg[1, j, rows(half[p] * HALF, HALF)], wi[j, cols(d)], 1, 1)
        if j == 0:
            dxf[p, d] = part
        else:
            dxf[p, d] += part
        if j == NJ - 1:
            for yy in range(4):
                dxss[p, d, yy] = dxf[p, d, rows((yy * 2 + oco) * TB, TB)].astype(BF16)
            dx_s(p, d).start()

    def tokens_middle(p, d):
        dx_s(p, d).wait_recv()
        for yy in range(4):
            part = dxf[p, d, rows((yy * 2 + co) * TB, TB)] + dxsr[p, d, yy].astype(F32)
            dxyf[p, d, yy] = part
            dxys[p, d, yy] = part.astype(BF16)
        for dy in (2, 1, 3):
            dx_y(p, d, dy).start()

    def tokens_sum(p, d):
        dx_y_all(p, d).wait_recv()
        value = dxyf[p, d, y]
        for i in range(3):
            value = value + dxyr[p, d, i].astype(F32)
        if p:
            dxcs[d] = value.astype(BF16)
            dx_c(d).start()
        else:
            dx_c(d).wait_recv()
            r_tok[:, cols(d)] = (value + dxcr[d].astype(F32)).astype(BF16)

    local = [pltpu.make_async_copy((tok, cot)[a], tslot(a, c, y, co), m_loc.at[a]) for a in range(2)]
    local += [pltpu.make_async_copy(wout.at[pl.ds(j * OB, OB)], wo.at[j, rows(x * OB, OB)], m_loc.at[2 + j]) for j in range(NJ)]
    columns = pltpu.make_async_copy(win, wl, m_loc.at[5])
    result_in = [pltpu.make_async_copy(r_win.at[i], o_win.at[:, pl.ds(i * HID, HID)], m_res.at[i]) for i in range(2)]
    columns.start()
    for copy in local:
        copy.start()
    barrier = pltpu.get_barrier_semaphore()
    partners = [dev(fs=1), dev(fc=1), dev(dk=1), dev(dk=3)]
    for d in (1, 2, 3):
        partners += [dev(dy=d), dev(dx=d)]
    for to in partners:
        pl.semaphore_signal(barrier, inc=1, device_id=to, device_id_type=MESH)
    columns.wait()
    for j in range(NJ):
        for cc in range(2):
            for xx in range(4):
                wst[cc, j, :, pl.ds(xx * OB, OB)] = wl[:, pl.ds(cc * HID + xx * WB + j * OB, OB)]
        wi[j, rows((c * 4 + x) * WB, WB)] = wst[c, j]
    pl.semaphore_wait(barrier, len(partners))

    wi_c(0).start()
    for d in (2, 1, 3):
        wi_x(0, 0, d).start()
        ag_y(0, 0, d).start()
    ag_c(0).start()
    ag_s(0, 0, 0).start()
    wi_c(1).start()
    wi_c(2).start()
    ag_c(1).start()
    wi_c(0).wait_recv()
    for d in (2, 1, 3):
        wi_x(0, 1, d).start()
    for r in range(2):
        wi_n(1, 0, r).start()
    ag_c(0).wait_recv()
    for d in (2, 1, 3):
        ag_y(0, 1, d).start()
    ag_s(0, 1, 0).start()
    for d in (1, 3, 2):
        ag_y(0, 0, d).wait_recv()
        ag_s(0, 0, d).start()
    wi_c(1).wait_recv()
    for r in range(2):
        wi_n(1, 1, r).start()
    for r in range(2):
        wi_n(2, 0, r).start()
    for copy in local:
        copy.wait()
    ag_s_all(0, 0).wait_recv()
    wi_x_all(0).wait_recv()
    product(0)
    wi_c(2).wait_recv()
    for r in range(2):
        wi_n(2, 1, r).start()
    for d in (1, 3, 2):
        ag_y(0, 1, d).wait_recv()
        ag_s(0, 1, d).start()
    wi_pass_on(1)
    for d in (2, 1, 3):
        ag_y(1, 0, d).start()
    ag_s(1, 0, 0).start()
    ag_c(1).wait_recv()
    for d in (2, 1, 3):
        ag_y(1, 1, d).start()
    ag_s(1, 1, 0).start()
    ag_s_all(0, 1).wait_recv()
    product(1)

    for t in range(1, 2 * NU + 4):
        if t - 1 < 2 * NU:
            middle(t - 1)
        if 0 <= t - 2 < 2 * NU:
            finish(t - 2)
        if 0 <= t - 3 < 2 * NU:
            forward(t - 3)
        if t == 1:
            wi_x_all(1).wait_recv()
        if t == 3:
            wi_x_all(2).wait_recv()
        if t == NU - 1:
            for p in (0, 1):
                ag_s_all(1, p).wait_recv()
        for j in range(NJ):
            if t + 1 == NU + (0, 2, 3)[j]:
                wo_all(j).wait_recv()
        if t + 1 < 2 * NU:
            product(t + 1)
        if t == 1:
            wo_send(0)
        if t == 2:
            wi_pass_on(2)
            wo_send(1)
        if t == 3:
            for p in (0, 1):
                for d in (1, 3, 2):
                    ag_y(1, p, d).wait_recv()
                    ag_s(1, p, d).start()
            wo_pass_on(0)
            wo_send(2)
        if t in (4, 5):
            wo_pass_on(t - 3)
        for j in range(NJ):
            if t == 2 * j + 5:
                arrived(2 * j)
                arrived(2 * j + 1)
                weight_out_part(j)
            if t == 2 * j + 6:
                weight_out_middle(j)
            if t == 2 * j + 8:
                weight_out_finish(j)
        u = t - 4
        if u >= NU:
            a, j, p = unit(u)
            arrived(u)
            if p:
                weight_in_half(j, 1)
            for d in range(ND):
                tokens_part(p, j, d)
            if not p:
                weight_in_part(j)
            if u == NU + 4:
                for d in range(ND):
                    tokens_middle(1, d)
    for d in range(ND):
        tokens_middle(0, d)
    weight_in_sum(0, 1)
    weight_in_sum(0, 0)
    for d in range(ND):
        tokens_sum(1, d)
    weight_in_sum(1, 1)
    weight_in_sum(1, 0)
    weight_in_sum(2, 1)
    for d in range(ND):
        tokens_sum(0, d)
    weight_in_sum(2, 0)
    for j in range(NJ):
        weight_in_finish(j)
    for copy in result_in:
        copy.start()

    whole = (
        tg.at[:, pl.ds(0, 15 * TB)], wi.at[:, pl.ds(0, 7 * WB)], wo.at[:, pl.ds(0, 3 * OB)], s1s, s2s,
        hg.at[:, :, pl.ds(0, 6 * OWN)], o1s, o2s, dwcs, dxss, dxyr, dxcs, dwis,
    )
    for family, ref in enumerate(whole):
        cp(ref, ref, family, m_agc.at[0], dev(fs=1)).wait_send()
    for copy in result_in:
        copy.wait()


def shards(tokens, cotangent, weight_in, weight_out):
    scale = float(tokens.shape[0] * lax.axis_size("out") * lax.axis_size("dep")) ** (-0.5)
    vmem, dma = pltpu.VMEM, pltpu.SemaphoreType.DMA
    hbm = pl.BlockSpec(memory_space=pl.ANY)
    own = pl.BlockSpec(memory_space=pltpu.VMEM)
    shapes = tuple(vmem(a.shape, BF16) for a in (tokens, weight_in, weight_out))
    return pl.pallas_call(
        functools.partial(kernel, scale),
        out_shape=shapes,
        in_specs=[hbm] * 4,
        out_specs=(own,) * 3,
        scratch_shapes=[
            vmem((2, TOK, WID), BF16),
            vmem((WB, 2 * HID), BF16),
            vmem((2, NJ, WB, CH), BF16),
            vmem((NJ, WID, CH), BF16),
            vmem((NJ, CH, WID), BF16),
            vmem((4, HALF, CH), F32),
            vmem((2 * NU, 2, 2, TB, CH), BF16),
            vmem((2 * NU, 2, 2, TB, CH), BF16),
            vmem((2 * NU, 2, TB, CH), BF16),
            vmem((2 * NU, 2, TB, CH), BF16),
            vmem((2, NJ, TOK, CH), BF16),
            vmem((NJ, 2, 2, TB, CH), F32),
            vmem((NJ, CH, WID), F32),
            vmem((NJ, 2, 2, OH, WID), BF16),
            vmem((NJ, 2, 2, OH, WID), BF16),
            vmem((NJ, 2, OH, WID), BF16),
            vmem((NJ, 2, OH, WID), BF16),
            vmem((NJ, WID, CH), F32),
            vmem((NJ, 2, 3, WB, CH), BF16),
            vmem((NJ, 2, 3, WB, CH), BF16),
            vmem((NJ, WB, CH), BF16),
            vmem((NJ, WB, CH), BF16),
            vmem((2, ND, HALF, DC), F32),
            vmem((2, ND, 4, TB, DC), BF16),
            vmem((2, ND, 4, TB, DC), BF16),
            vmem((2, ND, 4, TB, DC), F32),
            vmem((2, ND, 4, TB, DC), BF16),
            vmem((2, ND, 3, TB, DC), BF16),
            vmem((ND, TB, DC), BF16),
            vmem((ND, TB, DC), BF16),
            vmem((2, WB, HID), BF16),
            dma((6,)),
            dma((2,)),
            dma((15,)),
            dma((2,)),
            dma((2, 2, 3)),
            dma((2, 2)),
            dma((NJ,)),
            dma((NJ,)),
            dma((NJ, 2)),
            dma((NJ,)),
            dma((NJ, 2)),
            dma((2 * NU, 2)),
            dma((2 * NU, 2)),
            dma((2 * NU, 2)),
            dma((2 * NU, 2)),
            dma((NJ, 2)),
            dma((NJ, 2)),
            dma((NJ, 2)),
            dma((NJ,)),
            dma((2, ND)),
            dma((2, ND)),
            dma((ND,)),
        ],
        compiler_params=pltpu.CompilerParams(
            collective_id=0, has_side_effects=True, vmem_limit_bytes=61 * 2**20
        ),
        cost_estimate=pl.CostEstimate(flops=11 * 10**9, bytes_accessed=3 * 10**6, transcendentals=0),
    )(tokens, cotangent, weight_in, weight_out)


def solution(mesh):
    in_specs = (
        P(("dep", "out"), "inp"),
        P(("dep", "out"), "inp"),
        P(("inp", "dep"), "out"),
        P(("out", "dep"), "inp"),
    )
    out_specs = (P(("dep", "out"), "inp"), P(("inp", "dep"), "out"), P(("out", "dep"), "inp"))
    return jax.shard_map(shards, mesh=mesh, in_specs=in_specs, out_specs=out_specs, check_vma=False)
```

```python
import functools

import jax
import jax.numpy as jnp
from jax import lax
from jax.experimental import pallas as pl
from jax.experimental.pallas import tpu as pltpu
from jax.sharding import PartitionSpec as P

MESH = pl.DeviceIdType.MESH
BF16, F32 = jnp.bfloat16, jnp.float32
NJ, CH = 3, 256
NU = 2 * NJ
ORDER = ((0, 1), (0, 0), (1, 1), (2, 1), (1, 0), (2, 0))
ND, DC = 3, 512
OB, OH = 64, 32
STEP = (1, 3)
TB, WB = 48, 192
TOK, WID, HID = 768, 1536, 768
HALF, OWN = 384, 96


def dot(a, b, ca, cb):
    return lax.dot_general(a, b, (((ca,), (cb,)), ((), ())), preferred_element_type=F32)


def gelu_parts(preact):
    normal_cdf = 0.5 * (1.0 + lax.erf(preact * 0.7071067811865476))
    density = jnp.exp(-0.5 * preact * preact) * 0.3989422804014327
    return preact * normal_cdf, normal_cdf + preact * density


def kernel(
    scale, tok, cot, win, wout, r_tok, o_win, r_wout,
    tg, wl, wst, wi, wo, pf, s1s, s1r, s2s, s2r, hg, slope, dwof, o1s, o1r, o2s, o2r,
    dwif, dwis, dwir, dwcs, dwcr, dxf, dxss, dxsr, dxyf, dxys, dxyr, dxcs, dxcr,
    r_win, m_loc, m_res, sent, m_agc, m_agy, m_ags, m_wic, m_wix, m_wif, m_wox, m_wof, m_s1, m_s2, m_h1, m_h2,
    m_o1, m_o2, m_dwi, m_dwc, m_dxs, m_dxy, m_dxc,
):
    k, out, dep = lax.axis_index("inp"), lax.axis_index("out"), lax.axis_index("dep")
    y, co, c, x = out // 2, out % 2, dep // 4, dep % 4
    oc, oco = 1 - c, 1 - co
    half = (c, oc)

    def dev(dk=0, dy=0, dx=0, fc=0, fs=0):
        o = (y + dy) % 4 * 2 + (oco if fs else co)
        d = (oc if fc else c) * 4 + (x + dx) % 4
        return {"inp": (k + dk) % 4, "out": o, "dep": d}

    def cp(src, dst, family, recv, to):
        return pltpu.make_async_remote_copy(
            src_ref=src, dst_ref=dst, send_sem=sent.at[family], recv_sem=recv, device_id=to, device_id_type=MESH
        )

    def rows(start, n):
        return pl.ds(pl.multiple_of(start, 16), n)

    def tslot(a, cc, yy, oo):
        return tg.at[a, rows(((cc * 4 + yy) * 2 + oo) * TB, TB)]

    def ag_c(a):
        return cp((tok, cot)[a], tslot(a, c, y, co), 0, m_agc.at[a], dev(fc=1))

    def ag_y(a, p, dy):
        slot = tslot(a, half[p], y, co)
        return cp(slot if p else (tok, cot)[a], slot, 0, m_agy.at[a, p, dy - 1], dev(dy=dy))

    def ag_s(a, p, dy):
        slot = tslot(a, half[p], (y + 4 - dy) % 4, co)
        src = (tok, cot)[a] if (p == 0 and dy == 0) else slot
        return cp(src, slot, 0, m_ags.at[a, p], dev(fs=1))

    def ag_s_all(a, p):
        ref = tg.at[a, pl.ds(0, 4 * TB)]
        return cp(ref, ref, 0, m_ags.at[a, p], dev(fs=1))

    def wslot(j, cc, xx):
        return wi.at[j, rows((cc * 4 + xx) * WB, WB)]

    def wi_c(j):
        return cp(wst.at[oc, j], wslot(j, c, x), 1, m_wic.at[j], dev(fc=1))

    def wi_x(j, p, dx):
        slot = wslot(j, half[p], x)
        return cp(slot if p else wst.at[c, j], slot, 1, m_wix.at[j], dev(dx=dx))

    def wi_x_all(j):
        ref = wi.at[j, pl.ds(0, (4 if j else 6) * WB)]
        return cp(ref, ref, 1, m_wix.at[j], dev(dx=1))

    def wi_n(j, p, r):
        slot = wslot(j, half[p], x)
        sem = m_wif.at[j, p] if p == r else m_wix.at[j]
        return cp(slot if p else wst.at[c, j], slot, 1, sem, dev(dx=STEP[r]))

    def wi_f(j, p):
        slot = wslot(j, half[p], (x + STEP[1 - p]) % 4)
        return cp(slot, slot, 1, m_wix.at[j], dev(dx=STEP[p]))

    def wi_pass_on(j):
        slot = wslot(j, 0, 0)
        for p in range(2):
            cp(slot, slot, 1, m_wif.at[j, p], dev(dx=1)).wait_recv()
            wi_f(j, p).start()

    def wo_part(j, xx, part):
        return wo.at[j, rows(xx % 4 * OB + part * OH, OH)]

    def wo_n(j, r, part):
        sem = m_wof.at[j, r] if part == r else m_wox.at[j]
        src = wout.at[pl.ds(j * OB + part * OH, OH)]
        return cp(src, wo_part(j, x, part), 2, sem, dev(dx=STEP[r]))

    def wo_f(j, r):
        slot = wo_part(j, x + STEP[1 - r], r)
        return cp(slot, slot, 2, m_wox.at[j], dev(dx=STEP[r]))

    def wo_all(j):
        ref = wo.at[j, pl.ds(0, 4 * OH)]
        return cp(ref, ref, 2, m_wox.at[j], dev(dx=1))

    def wo_send(j):
        for i in range(2):
            for r in range(2):
                wo_n(j, r, (r + i) % 2).start()

    def wo_pass_on(j):
        for r in range(2):
            wo_n(j, r, r).wait_recv()
            wo_f(j, r).start()

    def unit(u):
        a, i = divmod(u, NU)
        return (a, *ORDER[i]) if a else (a, i // 2, i % 2)

    def s1(u, r):
        return cp(s1s.at[u, r, 0], s1r.at[u, r, 0], 3, m_s1.at[u, r], dev(dk=STEP[r]))

    def s1_own(u, r):
        return cp(s1s.at[u, r, 1], s1r.at[u, r, 1], 3, m_s2.at[u], dev(dk=STEP[r]))

    def s2(u, r):
        return cp(s2s.at[u, r], s2r.at[u, r], 4, m_s2.at[u], dev(dk=STEP[r]))

    def s2_all(u):
        return cp(s1r.at[u], s1r.at[u], 4, m_s2.at[u], dev(dk=1))

    def hrows(u, owner, part, n):
        a, j, p = unit(u)
        return hg.at[a, j, rows(half[p] * HALF + owner % 4 * OWN + part * TB, n)]

    def h1(u, r):
        slot = hrows(u, k, r, TB)
        return cp(slot, slot, 5, m_h1.at[u, r], dev(dk=STEP[r]))

    def h1_own(u, r):
        slot = hrows(u, k, 1 - r, TB)
        return cp(slot, slot, 5, m_h2.at[u], dev(dk=STEP[r]))

    def h2(u, r):
        slot = hrows(u, k + STEP[1 - r], r, TB)
        return cp(slot, slot, 5, m_h2.at[u], dev(dk=STEP[r]))

    def h2_all(u):
        ref = hg.at[0, 0, pl.ds(0, 4 * TB)]
        return cp(ref, ref, 5, m_h2.at[u], dev(dk=1))

    def o1(j, r):
        return cp(o1s.at[j, r], o1r.at[j, r], 6, m_o1.at[j, r], dev(dx=STEP[r]))

    def o2(j, r):
        return cp(o2s.at[j, r], o2r.at[j, r], 7, m_o2.at[j, r], dev(dx=STEP[r]))

    def dwi_x(j, p, dx):
        return cp(dwis.at[j, p, dx - 1], dwir.at[j, p, dx - 1], 12, m_dwi.at[j, p], dev(dx=dx))

    def dwi_x_all(j, p):
        return cp(dwir.at[j, p], dwir.at[j, p], 12, m_dwi.at[j, p], dev(dx=1))

    def dw_c(j):
        return cp(dwcs.at[j], dwcr.at[j], 8, m_dwc.at[j], dev(fc=1))

    def dx_s(p, d):
        return cp(dxss.at[p, d], dxsr.at[p, d], 9, m_dxs.at[p, d], dev(fs=1))

    def dx_y(p, d, dy):
        return cp(dxys.at[p, d, (y + dy) % 4], dxyr.at[p, d, dy - 1], 10, m_dxy.at[p, d], dev(dy=dy))

    def dx_y_all(p, d):
        return cp(dxyr.at[p, d], dxyr.at[p, d], 10, m_dxy.at[p, d], dev(dy=1))

    def dx_c(d):
        return cp(dxcs.at[d], dxcr.at[d], 11, m_dxc.at[d], dev(fc=1))

    def product(u):
        a, j, p = unit(u)
        lhs = tg[a, rows(half[p] * HALF, HALF)]
        pf[u % 4] = dot(lhs, wo[j], 1, 1) if a else dot(lhs, wi[j], 1, 0)

        def piece(owner, part):
            return pf[u % 4, rows(owner % 4 * OWN + part * TB, TB)].astype(BF16)

        for r in range(2):
            s1s[u, r, 0] = piece(k + 2, r)
            s1(u, r).start()
        for r in range(2):
            s1s[u, r, 1] = piece(k + STEP[r], 1 - r)
            s1_own(u, r).start()

    def middle(u):
        for r in range(2):
            s1(u, r).wait_recv()
            own = pf[u % 4, rows((k + STEP[r]) % 4 * OWN + r * TB, TB)]
            s2s[u, r] = (own + s1r[u, r, 0].astype(F32)).astype(BF16)
            s2(u, r).start()

    def finish(u):
        a, j, p = unit(u)
        s2_all(u).wait_recv()
        for r in range(2):
            value = pf[u % 4, rows(k * OWN + r * TB, TB)] + s2r[u, r].astype(F32) + s1r[u, 1 - r, 1].astype(F32)
            if a:
                value = value * slope[j, p, r]
            else:
                value, slope[j, p, r] = gelu_parts(value)
            hg[a, j, rows(half[p] * HALF + k * OWN + r * TB, TB)] = value.astype(BF16)
        for r in range(2):
            h1(u, r).start()

    def finish_sent(u):
        for r in range(2):
            h1_own(u, r).start()

    def forward(u):
        for r in range(2):
            h1(u, r).wait_recv()
            h2(u, r).start()

    def arrived(u):
        h2_all(u).wait_recv()

    def weight_out_part(j):
        dwof[j] = scale * dot(hg[0, j], tg[1], 0, 0)

        def piece(owner, part):
            return dwof[j, rows(owner % 4 * OB + part * OH, OH)].astype(BF16)

        for r in range(2):
            o1s[j, r, 0] = piece(x + 2, r)
            o1s[j, r, 1] = piece(x + STEP[r], 1 - r)
            o1(j, r).start()

    def weight_out_middle(j):
        for r in range(2):
            o1(j, r).wait_recv()
            own = dwof[j, rows((x + STEP[r]) % 4 * OB + r * OH, OH)]
            o2s[j, r] = (own + o1r[j, r, 0].astype(F32)).astype(BF16)
            o2(j, r).start()

    def weight_out_finish(j):
        for r in range(2):
            o2(j, r).wait_recv()
            value = dwof[j, rows(x * OB + r * OH, OH)] + o2r[j, r].astype(F32) + o1r[j, 1 - r, 1].astype(F32)
            r_wout[pl.ds(j * OB + r * OH, OH)] = value.astype(BF16)

    def weight_in_half(j, p):
        value = scale * dot(tg[0, rows(half[p] * HALF, HALF)], hg[1, j, rows(half[p] * HALF, HALF)], 0, 0)
        if p:
            dwif[j] = value
        else:
            dwif[j] += value

    def weight_in_piece(j, p, owner):
        return dwif[j, rows((half[p] * 4 + owner % 4) * WB, WB)]

    def weight_in_part(j):
        weight_in_half(j, 0)
        for p in (1, 0):
            for d in (2, 1, 3):
                dwis[j, p, d - 1] = weight_in_piece(j, p, x + d).astype(BF16)
                dwi_x(j, p, d).start()

    def weight_in_result(cc, j, value):
        for xx in range(4):
            r_win[cc, :, pl.ds(xx * WB + j * OB, OB)] = value[:, xx * OB : (xx + 1) * OB]

    def weight_in_sum(j, p):
        value = weight_in_piece(j, p, x)
        dwi_x_all(j, p).wait_recv()
        for d in range(3):
            value = value + dwir[j, p, d].astype(F32)
        if p:
            dwcs[j] = value.astype(BF16)
            dw_c(j).start()
        else:
            weight_in_result(c, j, value.astype(BF16))

    def weight_in_finish(j):
        dw_c(j).wait_recv()
        weight_in_result(oc, j, dwcr[j])

    def cols(d):
        return pl.ds(d * DC, DC)

    def tokens_part(p, j, d):
        part = dot(hg[1, j, rows(half[p] * HALF, HALF)], wi[j, cols(d)], 1, 1)
        if j == 0:
            dxf[p, d] = part
        else:
            dxf[p, d] += part
        if j == NJ - 1:
            for yy in range(4):
                dxss[p, d, yy] = dxf[p, d, rows((yy * 2 + oco) * TB, TB)].astype(BF16)
            dx_s(p, d).start()

    def tokens_middle(p, d):
        dx_s(p, d).wait_recv()
        for yy in range(4):
            part = dxf[p, d, rows((yy * 2 + co) * TB, TB)] + dxsr[p, d, yy].astype(F32)
            dxyf[p, d, yy] = part
            dxys[p, d, yy] = part.astype(BF16)
        for dy in (2, 1, 3):
            dx_y(p, d, dy).start()

    def tokens_sum(p, d):
        dx_y_all(p, d).wait_recv()
        value = dxyf[p, d, y]
        for i in range(3):
            value = value + dxyr[p, d, i].astype(F32)
        if p:
            dxcs[d] = value.astype(BF16)
            dx_c(d).start()
        else:
            dx_c(d).wait_recv()
            r_tok[:, cols(d)] = (value + dxcr[d].astype(F32)).astype(BF16)

    local = [pltpu.make_async_copy((tok, cot)[a], tslot(a, c, y, co), m_loc.at[a]) for a in range(2)]
    local += [pltpu.make_async_copy(wout.at[pl.ds(j * OB, OB)], wo.at[j, rows(x * OB, OB)], m_loc.at[2 + j]) for j in range(NJ)]
    columns = pltpu.make_async_copy(win, wl, m_loc.at[5])
    result_in = [pltpu.make_async_copy(r_win.at[i], o_win.at[:, pl.ds(i * HID, HID)], m_res.at[i]) for i in range(2)]
    columns.start()
    for copy in local:
        copy.start()
    barrier = pltpu.get_barrier_semaphore()
    partners = [dev(fs=1), dev(fc=1), dev(dk=1), dev(dk=3)]
    for d in (1, 2, 3):
        partners += [dev(dy=d), dev(dx=d)]
    for to in partners:
        pl.semaphore_signal(barrier, inc=1, device_id=to, device_id_type=MESH)
    columns.wait()
    for j in range(NJ):
        for cc in range(2):
            for xx in range(4):
                wst[cc, j, :, pl.ds(xx * OB, OB)] = wl[:, pl.ds(cc * HID + xx * WB + j * OB, OB)]
        wi[j, rows((c * 4 + x) * WB, WB)] = wst[c, j]
    pl.semaphore_wait(barrier, len(partners))

    wi_c(0).start()
    for d in (2, 1, 3):
        wi_x(0, 0, d).start()
        ag_y(0, 0, d).start()
    ag_c(0).start()
    ag_s(0, 0, 0).start()
    wi_c(1).start()
    wi_c(2).start()
    ag_c(1).start()
    wi_c(0).wait_recv()
    for d in (2, 1, 3):
        wi_x(0, 1, d).start()
    for r in range(2):
        wi_n(1, 0, r).start()
    ag_c(0).wait_recv()
    for d in (2, 1, 3):
        ag_y(0, 1, d).start()
    ag_s(0, 1, 0).start()
    for d in (1, 3, 2):
        ag_y(0, 0, d).wait_recv()
        ag_s(0, 0, d).start()
    wi_c(1).wait_recv()
    for r in range(2):
        wi_n(1, 1, r).start()
    for r in range(2):
        wi_n(2, 0, r).start()
    for copy in local:
        copy.wait()
    ag_s_all(0, 0).wait_recv()
    wi_x_all(0).wait_recv()
    product(0)
    wi_c(2).wait_recv()
    for r in range(2):
        wi_n(2, 1, r).start()
    for d in (1, 3, 2):
        ag_y(0, 1, d).wait_recv()
        ag_s(0, 1, d).start()
    wi_pass_on(1)
    for d in (2, 1, 3):
        ag_y(1, 0, d).start()
    ag_s(1, 0, 0).start()
    ag_c(1).wait_recv()
    for d in (2, 1, 3):
        ag_y(1, 1, d).start()
    ag_s(1, 1, 0).start()
    ag_s_all(0, 1).wait_recv()
    product(1)

    for t in range(1, 2 * NU + 4):
        if t - 1 < 2 * NU:
            middle(t - 1)
        if 0 <= t - 2 < 2 * NU:
            finish(t - 2)
        if 0 <= t - 3 < 2 * NU:
            forward(t - 3)
        if t == 1:
            wi_x_all(1).wait_recv()
        if t == 3:
            wi_x_all(2).wait_recv()
        if t == NU - 1:
            for p in (0, 1):
                ag_s_all(1, p).wait_recv()
        for j in range(NJ):
            if t + 1 == NU + (0, 2, 3)[j]:
                wo_all(j).wait_recv()
        if t + 1 < 2 * NU:
            product(t + 1)
        if 0 <= t - 2 < 2 * NU:
            finish_sent(t - 2)
        if t == 1:
            wo_send(0)
        if t == 2:
            wi_pass_on(2)
            wo_send(1)
        if t == 3:
            for p in (0, 1):
                for d in (1, 3, 2):
                    ag_y(1, p, d).wait_recv()
                    ag_s(1, p, d).start()
            wo_pass_on(0)
            wo_send(2)
        if t in (4, 5):
            wo_pass_on(t - 3)
        for j in range(NJ):
            if t == 2 * j + 5:
                arrived(2 * j)
                arrived(2 * j + 1)
                weight_out_part(j)
            if t == 2 * j + 6:
                weight_out_middle(j)
            if t == 2 * j + 8:
                weight_out_finish(j)
        u = t - 4
        if u >= NU:
            a, j, p = unit(u)
            arrived(u)
            if p:
                weight_in_half(j, 1)
            for d in range(ND):
                tokens_part(p, j, d)
            if not p:
                weight_in_part(j)
            if u == NU + 4:
                for d in range(ND):
                    tokens_middle(1, d)
    for d in range(ND):
        tokens_middle(0, d)
    weight_in_sum(0, 1)
    weight_in_sum(0, 0)
    for d in range(ND):
        tokens_sum(1, d)
    weight_in_sum(1, 1)
    weight_in_sum(1, 0)
    weight_in_sum(2, 1)
    for d in range(ND):
        tokens_sum(0, d)
    weight_in_sum(2, 0)
    for j in range(NJ):
        weight_in_finish(j)
    for copy in result_in:
        copy.start()

    whole = (
        tg.at[:, pl.ds(0, 15 * TB)], wi.at[:, pl.ds(0, 7 * WB)], wo.at[:, pl.ds(0, 3 * OB)], s1s, s2s,
        hg.at[:, :, pl.ds(0, 6 * OWN)], o1s, o2s, dwcs, dxss, dxyr, dxcs, dwis,
    )
    for family, ref in enumerate(whole):
        cp(ref, ref, family, m_agc.at[0], dev(fs=1)).wait_send()
    for copy in result_in:
        copy.wait()


def shards(tokens, cotangent, weight_in, weight_out):
    scale = float(tokens.shape[0] * lax.axis_size("out") * lax.axis_size("dep")) ** (-0.5)
    vmem, dma = pltpu.VMEM, pltpu.SemaphoreType.DMA
    hbm = pl.BlockSpec(memory_space=pl.ANY)
    own = pl.BlockSpec(memory_space=pltpu.VMEM)
    shapes = tuple(vmem(a.shape, BF16) for a in (tokens, weight_in, weight_out))
    return pl.pallas_call(
        functools.partial(kernel, scale),
        out_shape=shapes,
        in_specs=[hbm] * 4,
        out_specs=(own,) * 3,
        scratch_shapes=[
            vmem((2, TOK, WID), BF16),
            vmem((WB, 2 * HID), BF16),
            vmem((2, NJ, WB, CH), BF16),
            vmem((NJ, WID, CH), BF16),
            vmem((NJ, CH, WID), BF16),
            vmem((4, HALF, CH), F32),
            vmem((2 * NU, 2, 2, TB, CH), BF16),
            vmem((2 * NU, 2, 2, TB, CH), BF16),
            vmem((2 * NU, 2, TB, CH), BF16),
            vmem((2 * NU, 2, TB, CH), BF16),
            vmem((2, NJ, TOK, CH), BF16),
            vmem((NJ, 2, 2, TB, CH), F32),
            vmem((NJ, CH, WID), F32),
            vmem((NJ, 2, 2, OH, WID), BF16),
            vmem((NJ, 2, 2, OH, WID), BF16),
            vmem((NJ, 2, OH, WID), BF16),
            vmem((NJ, 2, OH, WID), BF16),
            vmem((NJ, WID, CH), F32),
            vmem((NJ, 2, 3, WB, CH), BF16),
            vmem((NJ, 2, 3, WB, CH), BF16),
            vmem((NJ, WB, CH), BF16),
            vmem((NJ, WB, CH), BF16),
            vmem((2, ND, HALF, DC), F32),
            vmem((2, ND, 4, TB, DC), BF16),
            vmem((2, ND, 4, TB, DC), BF16),
            vmem((2, ND, 4, TB, DC), F32),
            vmem((2, ND, 4, TB, DC), BF16),
            vmem((2, ND, 3, TB, DC), BF16),
            vmem((ND, TB, DC), BF16),
            vmem((ND, TB, DC), BF16),
            vmem((2, WB, HID), BF16),
            dma((6,)),
            dma((2,)),
            dma((15,)),
            dma((2,)),
            dma((2, 2, 3)),
            dma((2, 2)),
            dma((NJ,)),
            dma((NJ,)),
            dma((NJ, 2)),
            dma((NJ,)),
            dma((NJ, 2)),
            dma((2 * NU, 2)),
            dma((2 * NU,)),
            dma((2 * NU, 2)),
            dma((2 * NU,)),
            dma((NJ, 2)),
            dma((NJ, 2)),
            dma((NJ, 2)),
            dma((NJ,)),
            dma((2, ND)),
            dma((2, ND)),
            dma((ND,)),
        ],
        compiler_params=pltpu.CompilerParams(
            collective_id=0, has_side_effects=True, vmem_limit_bytes=61 * 2**20
        ),
        cost_estimate=pl.CostEstimate(flops=11 * 10**9, bytes_accessed=3 * 10**6, transcendentals=0),
    )(tokens, cotangent, weight_in, weight_out)


def solution(mesh):
    in_specs = (
        P(("dep", "out"), "inp"),
        P(("dep", "out"), "inp"),
        P(("inp", "dep"), "out"),
        P(("out", "dep"), "inp"),
    )
    out_specs = (P(("dep", "out"), "inp"), P(("inp", "dep"), "out"), P(("out", "dep"), "inp"))
    return jax.shard_map(shards, mesh=mesh, in_specs=in_specs, out_specs=out_specs, check_vma=False)
```

```python
import functools

import jax
import jax.numpy as jnp
from jax import lax
from jax.experimental import pallas as pl
from jax.experimental.pallas import tpu as pltpu
from jax.sharding import PartitionSpec as P

MESH = pl.DeviceIdType.MESH
BF16, F32 = jnp.bfloat16, jnp.float32
NJ, CH = 3, 256
NU = 2 * NJ
ORDER = ((0, 1), (0, 0), (1, 1), (2, 1), (1, 0), (2, 0))
ND, DC = 3, 512
OB, OH = 64, 32
STEP = (1, 3)
TB, WB = 48, 192
TOK, WID, HID = 768, 1536, 768
HALF, OWN = 384, 96


def dot(a, b, ca, cb):
    return lax.dot_general(a, b, (((ca,), (cb,)), ((), ())), preferred_element_type=F32)


def gelu_parts(preact):
    normal_cdf = 0.5 * (1.0 + lax.erf(preact * 0.7071067811865476))
    density = jnp.exp(-0.5 * preact * preact) * 0.3989422804014327
    return preact * normal_cdf, normal_cdf + preact * density


def kernel(
    scale, tok, cot, win, wout, r_tok, o_win, r_wout,
    tg, wl, wst, wi, wo, pf, s1s, s1r, s2s, s2r, hg, slope, dwof, o1s, o1r, o2s, o2r,
    dwif, dwis, dwir, dwcs, dwcr, dxf, dxss, dxsr, dxyf, dxys, dxyr, dxcs, dxcr,
    r_win, m_loc, m_res, sent, m_agc, m_agy, m_ags, m_wic, m_wix, m_wif, m_wox, m_wof, m_s1, m_s2, m_h1, m_h2,
    m_o1, m_o2, m_dwi, m_dwc, m_dxs, m_dxy, m_dxc,
):
    k, out, dep = lax.axis_index("inp"), lax.axis_index("out"), lax.axis_index("dep")
    y, co, c, x = out // 2, out % 2, dep // 4, dep % 4
    oc, oco = 1 - c, 1 - co
    half = (c, oc)

    def dev(dk=0, dy=0, dx=0, fc=0, fs=0):
        o = (y + dy) % 4 * 2 + (oco if fs else co)
        d = (oc if fc else c) * 4 + (x + dx) % 4
        return {"inp": (k + dk) % 4, "out": o, "dep": d}

    def cp(src, dst, family, recv, to):
        return pltpu.make_async_remote_copy(
            src_ref=src, dst_ref=dst, send_sem=sent.at[family], recv_sem=recv, device_id=to, device_id_type=MESH
        )

    def rows(start, n):
        return pl.ds(pl.multiple_of(start, 16), n)

    def tslot(a, cc, yy, oo):
        return tg.at[a, rows(((cc * 4 + yy) * 2 + oo) * TB, TB)]

    def ag_c(a):
        return cp((tok, cot)[a], tslot(a, c, y, co), 0, m_agc.at[a], dev(fc=1))

    def ag_y(a, p, dy):
        slot = tslot(a, half[p], y, co)
        return cp(slot if p else (tok, cot)[a], slot, 0, m_agy.at[a, p, dy - 1], dev(dy=dy))

    def ag_s(a, p, dy):
        slot = tslot(a, half[p], (y + 4 - dy) % 4, co)
        src = (tok, cot)[a] if (p == 0 and dy == 0) else slot
        return cp(src, slot, 0, m_ags.at[a, p], dev(fs=1))

    def ag_s_all(a, p):
        ref = tg.at[a, pl.ds(0, 4 * TB)]
        return cp(ref, ref, 0, m_ags.at[a, p], dev(fs=1))

    def wslot(j, cc, xx):
        return wi.at[j, rows((cc * 4 + xx) * WB, WB)]

    def wi_c(j):
        return cp(wst.at[oc, j], wslot(j, c, x), 1, m_wic.at[j], dev(fc=1))

    def wi_x(j, p, dx):
        slot = wslot(j, half[p], x)
        return cp(slot if p else wst.at[c, j], slot, 1, m_wix.at[j], dev(dx=dx))

    def wi_x_all(j):
        ref = wi.at[j, pl.ds(0, (4 if j else 6) * WB)]
        return cp(ref, ref, 1, m_wix.at[j], dev(dx=1))

    def wi_n(j, p, r):
        slot = wslot(j, half[p], x)
        sem = m_wif.at[j, p] if p == r else m_wix.at[j]
        return cp(slot if p else wst.at[c, j], slot, 1, sem, dev(dx=STEP[r]))

    def wi_f(j, p):
        slot = wslot(j, half[p], (x + STEP[1 - p]) % 4)
        return cp(slot, slot, 1, m_wix.at[j], dev(dx=STEP[p]))

    def wi_pass_on(j):
        slot = wslot(j, 0, 0)
        for p in range(2):
            cp(slot, slot, 1, m_wif.at[j, p], dev(dx=1)).wait_recv()
            wi_f(j, p).start()

    def wo_part(j, xx, part):
        return wo.at[j, rows(xx % 4 * OB + part * OH, OH)]

    def wo_n(j, r, part):
        sem = m_wof.at[j, r] if part == r else m_wox.at[j]
        src = wout.at[pl.ds(j * OB + part * OH, OH)]
        return cp(src, wo_part(j, x, part), 2, sem, dev(dx=STEP[r]))

    def wo_f(j, r):
        slot = wo_part(j, x + STEP[1 - r], r)
        return cp(slot, slot, 2, m_wox.at[j], dev(dx=STEP[r]))

    def wo_all(j):
        ref = wo.at[j, pl.ds(0, 4 * OH)]
        return cp(ref, ref, 2, m_wox.at[j], dev(dx=1))

    def wo_send(j):
        for i in range(2):
            for r in range(2):
                wo_n(j, r, (r + i) % 2).start()

    def wo_pass_on(j):
        for r in range(2):
            wo_n(j, r, r).wait_recv()
            wo_f(j, r).start()

    def unit(u):
        a, i = divmod(u, NU)
        return (a, *ORDER[i]) if a else (a, i // 2, i % 2)

    def s1(u, r):
        return cp(s1s.at[u, r, 0], s1r.at[u, r, 0], 3, m_s1.at[u, r], dev(dk=STEP[r]))

    def s1_own(u, r):
        return cp(s1s.at[u, r, 1], s1r.at[u, r, 1], 3, m_s2.at[u], dev(dk=STEP[r]))

    def s2(u, r):
        return cp(s2s.at[u, r], s2r.at[u, r], 4, m_s2.at[u], dev(dk=STEP[r]))

    def s2_all(u):
        return cp(s1r.at[u], s1r.at[u], 4, m_s2.at[u], dev(dk=1))

    def hrows(u, owner, part, n):
        a, j, p = unit(u)
        return hg.at[a, j, rows(half[p] * HALF + owner % 4 * OWN + part * TB, n)]

    def h1(u, r):
        slot = hrows(u, k, r, TB)
        return cp(slot, slot, 5, m_h1.at[u, r], dev(dk=STEP[r]))

    def h1_own(u, r):
        slot = hrows(u, k, 1 - r, TB)
        return cp(slot, slot, 5, m_h2.at[u], dev(dk=STEP[r]))

    def h2(u, r):
        slot = hrows(u, k + STEP[1 - r], r, TB)
        return cp(slot, slot, 5, m_h2.at[u], dev(dk=STEP[r]))

    def h2_all(u):
        ref = hg.at[0, 0, pl.ds(0, 4 * TB)]
        return cp(ref, ref, 5, m_h2.at[u], dev(dk=1))

    def o1(j, r):
        return cp(o1s.at[j, r, 0], o1r.at[j, r, 0], 6, m_o1.at[j, r], dev(dx=STEP[r]))

    def o1_own(j, r):
        return cp(o1s.at[j, r, 1], o1r.at[j, r, 1], 6, m_o2.at[j], dev(dx=STEP[r]))

    def o2(j, r):
        return cp(o2s.at[j, r], o2r.at[j, r], 7, m_o2.at[j], dev(dx=STEP[r]))

    def o2_all(j):
        return cp(o1r.at[j], o1r.at[j], 7, m_o2.at[j], dev(dx=1))

    def dwi_x(j, p, dx):
        return cp(dwis.at[j, p, dx - 1], dwir.at[j, p, dx - 1], 12, m_dwi.at[j, p], dev(dx=dx))

    def dwi_x_all(j, p):
        return cp(dwir.at[j, p], dwir.at[j, p], 12, m_dwi.at[j, p], dev(dx=1))

    def dw_c(j):
        return cp(dwcs.at[j], dwcr.at[j], 8, m_dwc.at[j], dev(fc=1))

    def dx_s(p, d):
        return cp(dxss.at[p, d], dxsr.at[p, d], 9, m_dxs.at[p, d], dev(fs=1))

    def dx_y(p, d, dy):
        return cp(dxys.at[p, d, (y + dy) % 4], dxyr.at[p, d, dy - 1], 10, m_dxy.at[p, d], dev(dy=dy))

    def dx_y_all(p, d):
        return cp(dxyr.at[p, d], dxyr.at[p, d], 10, m_dxy.at[p, d], dev(dy=1))

    def dx_c(d):
        return cp(dxcs.at[d], dxcr.at[d], 11, m_dxc.at[d], dev(fc=1))

    def product(u):
        a, j, p = unit(u)
        lhs = tg[a, rows(half[p] * HALF, HALF)]
        pf[u % 4] = dot(lhs, wo[j], 1, 1) if a else dot(lhs, wi[j], 1, 0)

        def piece(owner, part):
            return pf[u % 4, rows(owner % 4 * OWN + part * TB, TB)].astype(BF16)

        for r in range(2):
            s1s[u, r, 0] = piece(k + 2, r)
            s1(u, r).start()
        for r in range(2):
            s1s[u, r, 1] = piece(k + STEP[r], 1 - r)
            s1_own(u, r).start()

    def middle(u):
        for r in range(2):
            s1(u, r).wait_recv()
            own = pf[u % 4, rows((k + STEP[r]) % 4 * OWN + r * TB, TB)]
            s2s[u, r] = (own + s1r[u, r, 0].astype(F32)).astype(BF16)
            s2(u, r).start()

    def finish(u):
        a, j, p = unit(u)
        s2_all(u).wait_recv()
        for r in range(2):
            value = pf[u % 4, rows(k * OWN + r * TB, TB)] + s2r[u, r].astype(F32) + s1r[u, 1 - r, 1].astype(F32)
            if a:
                value = value * slope[j, p, r]
            else:
                value, slope[j, p, r] = gelu_parts(value)
            hg[a, j, rows(half[p] * HALF + k * OWN + r * TB, TB)] = value.astype(BF16)
        for r in range(2):
            h1(u, r).start()

    def finish_sent(u):
        for r in range(2):
            h1_own(u, r).start()

    def forward(u):
        for r in range(2):
            h1(u, r).wait_recv()
            h2(u, r).start()

    def arrived(u):
        h2_all(u).wait_recv()

    def weight_out_part(j):
        dwof[j] = scale * dot(hg[0, j], tg[1], 0, 0)

        def piece(owner, part):
            return dwof[j, rows(owner % 4 * OB + part * OH, OH)].astype(BF16)

        for r in range(2):
            o1s[j, r, 0] = piece(x + 2, r)
            o1(j, r).start()
        for r in range(2):
            o1s[j, r, 1] = piece(x + STEP[r], 1 - r)
            o1_own(j, r).start()

    def weight_out_middle(j):
        for r in range(2):
            o1(j, r).wait_recv()
            own = dwof[j, rows((x + STEP[r]) % 4 * OB + r * OH, OH)]
            o2s[j, r] = (own + o1r[j, r, 0].astype(F32)).astype(BF16)
            o2(j, r).start()

    def weight_out_finish(j):
        o2_all(j).wait_recv()
        for r in range(2):
            value = dwof[j, rows(x * OB + r * OH, OH)] + o2r[j, r].astype(F32) + o1r[j, 1 - r, 1].astype(F32)
            r_wout[pl.ds(j * OB + r * OH, OH)] = value.astype(BF16)

    def weight_in_half(j, p):
        value = scale * dot(tg[0, rows(half[p] * HALF, HALF)], hg[1, j, rows(half[p] * HALF, HALF)], 0, 0)
        if p:
            dwif[j] = value
        else:
            dwif[j] += value

    def weight_in_piece(j, p, owner):
        return dwif[j, rows((half[p] * 4 + owner % 4) * WB, WB)]

    def weight_in_part(j):
        weight_in_half(j, 0)
        for p in (1, 0):
            for d in (2, 1, 3):
                dwis[j, p, d - 1] = weight_in_piece(j, p, x + d).astype(BF16)
                dwi_x(j, p, d).start()

    def weight_in_result(cc, j, value):
        for xx in range(4):
            r_win[cc, :, pl.ds(xx * WB + j * OB, OB)] = value[:, xx * OB : (xx + 1) * OB]

    def weight_in_sum(j, p):
        value = weight_in_piece(j, p, x)
        dwi_x_all(j, p).wait_recv()
        for d in range(3):
            value = value + dwir[j, p, d].astype(F32)
        if p:
            dwcs[j] = value.astype(BF16)
            dw_c(j).start()
        else:
            weight_in_result(c, j, value.astype(BF16))

    def weight_in_finish(j):
        dw_c(j).wait_recv()
        weight_in_result(oc, j, dwcr[j])

    def cols(d):
        return pl.ds(d * DC, DC)

    def tokens_part(p, j, d):
        part = dot(hg[1, j, rows(half[p] * HALF, HALF)], wi[j, cols(d)], 1, 1)
        if j == 0:
            dxf[p, d] = part
        else:
            dxf[p, d] += part
        if j == NJ - 1:
            for yy in range(4):
                dxss[p, d, yy] = dxf[p, d, rows((yy * 2 + oco) * TB, TB)].astype(BF16)
            dx_s(p, d).start()

    def tokens_middle(p, d):
        dx_s(p, d).wait_recv()
        for yy in range(4):
            part = dxf[p, d, rows((yy * 2 + co) * TB, TB)] + dxsr[p, d, yy].astype(F32)
            dxyf[p, d, yy] = part
            dxys[p, d, yy] = part.astype(BF16)
        for dy in (2, 1, 3):
            dx_y(p, d, dy).start()

    def tokens_sum(p, d):
        dx_y_all(p, d).wait_recv()
        value = dxyf[p, d, y]
        for i in range(3):
            value = value + dxyr[p, d, i].astype(F32)
        if p:
            dxcs[d] = value.astype(BF16)
            dx_c(d).start()
        else:
            dx_c(d).wait_recv()
            r_tok[:, cols(d)] = (value + dxcr[d].astype(F32)).astype(BF16)

    local = [pltpu.make_async_copy((tok, cot)[a], tslot(a, c, y, co), m_loc.at[a]) for a in range(2)]
    local += [pltpu.make_async_copy(wout.at[pl.ds(j * OB, OB)], wo.at[j, rows(x * OB, OB)], m_loc.at[2 + j]) for j in range(NJ)]
    columns = pltpu.make_async_copy(win, wl, m_loc.at[5])
    result_in = [pltpu.make_async_copy(r_win.at[i], o_win.at[:, pl.ds(i * HID, HID)], m_res.at[i]) for i in range(2)]
    columns.start()
    for copy in local:
        copy.start()
    barrier = pltpu.get_barrier_semaphore()
    partners = [dev(fs=1), dev(fc=1), dev(dk=1), dev(dk=3)]
    for d in (1, 2, 3):
        partners += [dev(dy=d), dev(dx=d)]
    for to in partners:
        pl.semaphore_signal(barrier, inc=1, device_id=to, device_id_type=MESH)
    columns.wait()
    for j in range(NJ):
        for cc in range(2):
            for xx in range(4):
                wst[cc, j, :, pl.ds(xx * OB, OB)] = wl[:, pl.ds(cc * HID + xx * WB + j * OB, OB)]
        wi[j, rows((c * 4 + x) * WB, WB)] = wst[c, j]
    pl.semaphore_wait(barrier, len(partners))

    wi_c(0).start()
    for d in (2, 1, 3):
        wi_x(0, 0, d).start()
        ag_y(0, 0, d).start()
    ag_c(0).start()
    ag_s(0, 0, 0).start()
    wi_c(1).start()
    wi_c(2).start()
    ag_c(1).start()
    wi_c(0).wait_recv()
    for d in (2, 1, 3):
        wi_x(0, 1, d).start()
    for r in range(2):
        wi_n(1, 0, r).start()
    ag_c(0).wait_recv()
    for d in (2, 1, 3):
        ag_y(0, 1, d).start()
    ag_s(0, 1, 0).start()
    for d in (1, 3, 2):
        ag_y(0, 0, d).wait_recv()
        ag_s(0, 0, d).start()
    wi_c(1).wait_recv()
    for r in range(2):
        wi_n(1, 1, r).start()
    for r in range(2):
        wi_n(2, 0, r).start()
    for copy in local:
        copy.wait()
    ag_s_all(0, 0).wait_recv()
    wi_x_all(0).wait_recv()
    product(0)
    wi_c(2).wait_recv()
    for r in range(2):
        wi_n(2, 1, r).start()
    for d in (1, 3, 2):
        ag_y(0, 1, d).wait_recv()
        ag_s(0, 1, d).start()
    wi_pass_on(1)
    for d in (2, 1, 3):
        ag_y(1, 0, d).start()
    ag_s(1, 0, 0).start()
    ag_c(1).wait_recv()
    for d in (2, 1, 3):
        ag_y(1, 1, d).start()
    ag_s(1, 1, 0).start()
    ag_s_all(0, 1).wait_recv()
    product(1)

    for t in range(1, 2 * NU + 4):
        if t - 1 < 2 * NU:
            middle(t - 1)
        if 0 <= t - 2 < 2 * NU:
            finish(t - 2)
        if 0 <= t - 3 < 2 * NU:
            forward(t - 3)
        if t == 1:
            wi_x_all(1).wait_recv()
        if t == 3:
            wi_x_all(2).wait_recv()
        if t == NU - 1:
            for p in (0, 1):
                ag_s_all(1, p).wait_recv()
        for j in range(NJ):
            if t + 1 == NU + (0, 2, 3)[j]:
                wo_all(j).wait_recv()
        if t + 1 < 2 * NU:
            product(t + 1)
        if 0 <= t - 2 < 2 * NU:
            finish_sent(t - 2)
        if t == 1:
            wo_send(0)
        if t == 2:
            wi_pass_on(2)
            wo_send(1)
        if t == 3:
            for p in (0, 1):
                for d in (1, 3, 2):
                    ag_y(1, p, d).wait_recv()
                    ag_s(1, p, d).start()
            wo_pass_on(0)
            wo_send(2)
        if t in (4, 5):
            wo_pass_on(t - 3)
        for j in range(NJ):
            if t == 2 * j + 5:
                arrived(2 * j)
                arrived(2 * j + 1)
                weight_out_part(j)
            if t == 2 * j + 6:
                weight_out_middle(j)
            if t == 2 * j + 8:
                weight_out_finish(j)
        u = t - 4
        if u >= NU:
            a, j, p = unit(u)
            arrived(u)
            if p:
                weight_in_half(j, 1)
            for d in range(ND):
                tokens_part(p, j, d)
            if not p:
                weight_in_part(j)
            if u == NU + 4:
                for d in range(ND):
                    tokens_middle(1, d)
    for d in range(ND):
        tokens_middle(0, d)
    weight_in_sum(0, 1)
    weight_in_sum(0, 0)
    for d in range(ND):
        tokens_sum(1, d)
    weight_in_sum(1, 1)
    weight_in_sum(1, 0)
    weight_in_sum(2, 1)
    for d in range(ND):
        tokens_sum(0, d)
    weight_in_sum(2, 0)
    for j in range(NJ):
        weight_in_finish(j)
    for copy in result_in:
        copy.start()

    whole = (
        tg.at[:, pl.ds(0, 15 * TB)], wi.at[:, pl.ds(0, 7 * WB)], wo.at[:, pl.ds(0, 3 * OB)], s1s, s2s,
        hg.at[:, :, pl.ds(0, 6 * OWN)], o1s, o2s, dwcs, dxss, dxyr, dxcs, dwis,
    )
    for family, ref in enumerate(whole):
        cp(ref, ref, family, m_agc.at[0], dev(fs=1)).wait_send()
    for copy in result_in:
        copy.wait()


def shards(tokens, cotangent, weight_in, weight_out):
    scale = float(tokens.shape[0] * lax.axis_size("out") * lax.axis_size("dep")) ** (-0.5)
    vmem, dma = pltpu.VMEM, pltpu.SemaphoreType.DMA
    hbm = pl.BlockSpec(memory_space=pl.ANY)
    own = pl.BlockSpec(memory_space=pltpu.VMEM)
    shapes = tuple(vmem(a.shape, BF16) for a in (tokens, weight_in, weight_out))
    return pl.pallas_call(
        functools.partial(kernel, scale),
        out_shape=shapes,
        in_specs=[hbm] * 4,
        out_specs=(own,) * 3,
        scratch_shapes=[
            vmem((2, TOK, WID), BF16),
            vmem((WB, 2 * HID), BF16),
            vmem((2, NJ, WB, CH), BF16),
            vmem((NJ, WID, CH), BF16),
            vmem((NJ, CH, WID), BF16),
            vmem((4, HALF, CH), F32),
            vmem((2 * NU, 2, 2, TB, CH), BF16),
            vmem((2 * NU, 2, 2, TB, CH), BF16),
            vmem((2 * NU, 2, TB, CH), BF16),
            vmem((2 * NU, 2, TB, CH), BF16),
            vmem((2, NJ, TOK, CH), BF16),
            vmem((NJ, 2, 2, TB, CH), F32),
            vmem((NJ, CH, WID), F32),
            vmem((NJ, 2, 2, OH, WID), BF16),
            vmem((NJ, 2, 2, OH, WID), BF16),
            vmem((NJ, 2, OH, WID), BF16),
            vmem((NJ, 2, OH, WID), BF16),
            vmem((NJ, WID, CH), F32),
            vmem((NJ, 2, 3, WB, CH), BF16),
            vmem((NJ, 2, 3, WB, CH), BF16),
            vmem((NJ, WB, CH), BF16),
            vmem((NJ, WB, CH), BF16),
            vmem((2, ND, HALF, DC), F32),
            vmem((2, ND, 4, TB, DC), BF16),
            vmem((2, ND, 4, TB, DC), BF16),
            vmem((2, ND, 4, TB, DC), F32),
            vmem((2, ND, 4, TB, DC), BF16),
            vmem((2, ND, 3, TB, DC), BF16),
            vmem((ND, TB, DC), BF16),
            vmem((ND, TB, DC), BF16),
            vmem((2, WB, HID), BF16),
            dma((6,)),
            dma((2,)),
            dma((15,)),
            dma((2,)),
            dma((2, 2, 3)),
            dma((2, 2)),
            dma((NJ,)),
            dma((NJ,)),
            dma((NJ, 2)),
            dma((NJ,)),
            dma((NJ, 2)),
            dma((2 * NU, 2)),
            dma((2 * NU,)),
            dma((2 * NU, 2)),
            dma((2 * NU,)),
            dma((NJ, 2)),
            dma((NJ,)),
            dma((NJ, 2)),
            dma((NJ,)),
            dma((2, ND)),
            dma((2, ND)),
            dma((ND,)),
        ],
        compiler_params=pltpu.CompilerParams(
            collective_id=0, has_side_effects=True, vmem_limit_bytes=61 * 2**20
        ),
        cost_estimate=pl.CostEstimate(flops=11 * 10**9, bytes_accessed=3 * 10**6, transcendentals=0),
    )(tokens, cotangent, weight_in, weight_out)


def solution(mesh):
    in_specs = (
        P(("dep", "out"), "inp"),
        P(("dep", "out"), "inp"),
        P(("inp", "dep"), "out"),
        P(("out", "dep"), "inp"),
    )
    out_specs = (P(("dep", "out"), "inp"), P(("inp", "dep"), "out"), P(("out", "dep"), "inp"))
    return jax.shard_map(shards, mesh=mesh, in_specs=in_specs, out_specs=out_specs, check_vma=False)
```
